256 devices in a mesh: section: 16 (over z_hi, x, core), tensor: 16 (over y, z_lo).
Axes of the slice: x: 4, y: 4, z: 8 (z_hi: 2, z_lo: 4; z = z_hi * 4 + z_lo), core: 2. Of those that a mesh axis runs over, the one named last changes fastest.
Arguments:
- hidden: bfloat16 [256, 16384], P('section', 'tensor'), as said below
- head_weight: bfloat16 [45056, 16384], P(('section', 'tensor')), as said below
- targets: int32 [256], replicated, may hold values from 0 to 45055
- loss_weight: float32 [256], replicated, may hold values from 0.5 to 4
Outputs:
- token_loss: float32 [256], replicated
- grad_weight: bfloat16 [45056, 16384], P(('section', 'tensor'))
- grad_hidden: bfloat16 [256, 16384], P('section', 'tensor')
The draws below stay inside these ranges and needn't reach their ends.
Inputs may be any that keep to these rules, and one draw needn't show every extreme that they name: hidden entries lie within -16 and 16. head_weight entries lie within -18 / sqrt(16384) and 18 / sqrt(16384).
All inputs are finite; a program needn't handle non-finite values.
Results may differ from the reference program's by a relative error of at most 0.0046.
Values may be sent and summed in bfloat16 or wider, within the bound.
A program may use at most 128 MiB of HBM per device.

```python
import math
import jax
import jax.numpy as jnp
from jax import lax

D = 16384
TOK = 256
VOC = 45056


def base_weight(key):
    return jnp.clip(jax.random.normal(key, (VOC, D), jnp.float32), -6.0, 6.0) * (3.0 / math.sqrt(D))


def draw_head_weight(key, part):
    return base_weight(key).astype(jnp.bfloat16)


def draw_hidden(key, part):
    own = jax.random.fold_in(key, 7)
    rows_drawn = jnp.clip(jax.random.normal(own, (TOK, D), jnp.float32), -6.0, 6.0)
    return rows_drawn.astype(jnp.bfloat16)


def with_ends(values, stream_key, smallest, top_value):
    longest = values.shape.index(max(values.shape))
    spots = []
    for shift in (0, 1):
        where = [jax.random.randint(jax.random.fold_in(stream_key, axis), (), 0, length) for axis, length in enumerate(values.shape)]
        where[longest] = (where[longest] + shift) % values.shape[longest]
        spots.append(tuple(where))
    return values.at[spots[0]].set(smallest).at[spots[1]].set(top_value)


def setup_inputs(seed: int = 0) -> dict:
    key_list = jax.random.split(jax.random.key(seed), 5)
    hidden = draw_hidden(jax.random.fold_in(key_list[4], 71), 0)
    head_weight = draw_head_weight(jax.random.fold_in(key_list[4], 71), 0)
    targets = with_ends(jax.random.randint(key_list[2], (TOK,), 0, VOC), jax.random.fold_in(key_list[2], 1), 0, VOC - 1).astype(jnp.int32)
    loss_weight = jnp.clip(jnp.exp(jax.random.uniform(key_list[3], (TOK,), jnp.float32, math.log(0.5), math.log(4.0))), 0.5, 4.0)
    return {"hidden": hidden, "head_weight": head_weight, "targets": targets, "loss_weight": loss_weight}


def reference(hidden, head_weight, targets, loss_weight):
    logits = lax.dot_general(hidden, head_weight, (((1,), (1,)), ((), ())), preferred_element_type=jnp.float32)
    row_top = jnp.max(logits, axis=1)
    row_total = jnp.sum(jnp.exp(logits - row_top[:, None]), axis=1)
    columns = jnp.arange(logits.shape[1], dtype=jnp.int32)
    hit = columns[None, :] == targets[:, None]
    picked = jnp.sum(jnp.where(hit, logits, jnp.float32(0.0)), axis=1)
    lse = row_top + jnp.log(row_total)
    token_loss = lse - picked
    dlogits = (loss_weight[:, None] * (jnp.exp(logits - lse[:, None]) - hit.astype(jnp.float32))).astype(jnp.bfloat16)
    grad_weight = lax.dot_general(dlogits, hidden, (((0,), (0,)), ((), ())), preferred_element_type=jnp.float32).astype(jnp.bfloat16)
    grad_hidden = jnp.dot(dlogits, head_weight, preferred_element_type=jnp.float32).astype(jnp.bfloat16)
    return token_loss, grad_weight, grad_hidden
```

```python
import jax
import jax.numpy as jnp
from jax import lax
from jax.experimental import pallas as pl
from jax.experimental.pallas import tpu as pltpu
from jax.sharding import PartitionSpec as P

MESH = pl.DeviceIdType.MESH
F32, BF16 = jnp.float32, jnp.bfloat16
SIZE = {"x": 4, "y": 4, "z": 8, "a": 4, "b": 4}
ZH, ZL = 2, 4
NB = SIZE["y"] * ZL
NQ = ZH * SIZE["x"]
ROWS = 16
FULL, HALF = 1024, 512
STREAMS = (
    (("z", "b", "a"), 0, 256),
    (("z", "a", "b"), 256, 128),
    (("y", "x", "z"), 384, 128),
)
NS = len(STREAMS)
WIDE = {"z": (0, 384), "y": (384, 128)}
LONG = [i for i in range(NS) if STREAMS[i][0][2] == "z"]
SHORT = [i for i in range(NS) if i not in LONG]
BLOCKS = 4


def lead(order):
    f, m, l = (SIZE[a] for a in order)
    return (l, m, f)


def hops(order, p):
    return SIZE[order[p]] // 2


class Kernel:
    def __init__(self, shard, refs):
        self.shard = shard
        self.__dict__.update(refs)
        sec, ten = lax.axis_index("section"), lax.axis_index("tensor")
        self.core = lax.rem(sec, 2)
        z = (sec // 8) * 4 + lax.rem(ten, 4)
        x, y = lax.rem(sec // 2, 4), ten // 4
        self.me = {"x": x, "y": y, "z": z} | self.roles(x, y)
        self.vocab0 = ((sec - self.core) * 16 + ten) * shard
        self.sends = []

    def roles(self, x, y):
        return {"a": jnp.where(self.core == 0, y, x), "b": jnp.where(self.core == 0, x, y)}

    def dev(self, core=None, **move):
        c = dict(self.me)
        for a, d in move.items():
            c[a] = lax.rem(c[a] + d + SIZE[a], SIZE[a])
            if a in ("a", "b"):
                first = self.core == (0 if a == "b" else 1)
                c["x"], c["y"] = jnp.where(first, c[a], c["x"]), jnp.where(first, c["y"], c[a])
        core = self.core if core is None else core
        return ((c["z"] // 4) * 8 + c["x"] * 2 + core, c["y"] * 4 + lax.rem(c["z"], 4))

    def remote(self, src, dst, ssem, rsem, device):
        return pltpu.make_async_remote_copy(
            src_ref=src, dst_ref=dst, send_sem=ssem, recv_sem=rsem, device_id=device, device_id_type=MESH
        )

    def send(self, *args):
        copy = self.remote(*args)
        copy.start()
        self.sends.append(copy)
        return copy

    def spread_copy(self, a, r, d):
        n = SIZE[a]
        col, width = WIDE[a]
        other = 1 - self.core
        to_core = other if r else self.core
        src = self.hid.at[:, pl.ds(pl.multiple_of(to_core * HALF + col, 128), width)]
        buf, sem = self.first[a], self.first_sem[a]
        if r == 0 and d == 0:
            return pltpu.make_async_copy(src, buf.at[self.core, self.me[a]], sem.at[1, 0, 0]), None
        dev = self.dev(core=to_core, **{a: d})
        sems = (sem.at[0, r, d], sem.at[1, r, d], dev)
        got = buf.at[to_core, lax.rem(self.me[a] - d + n, n)]
        return self.remote(src, buf.at[self.core, self.me[a]], *sems), self.remote(src, got, *sems)

    def spread(self):
        for a in ("z", "y"):
            for d in range(SIZE[a]):
                for r in (0, 1):
                    if d or r:
                        copy, _ = self.spread_copy(a, r, d)
                        copy.start()
                        self.sends.append(copy)

    def spread_wait(self):
        for a in ("z", "y"):
            for d in range(SIZE[a]):
                for r in (0, 1):
                    local, got = self.spread_copy(a, r, d)
                    if got is None:
                        local.wait()
                    else:
                        got.wait_recv()

    def gather_copy(self, i, p, way, kind, hop):
        order = STREAMS[i][0]
        a = order[p]
        n, w = SIZE[a], SIZE[order[p - 1]] // 2
        sign = 1 - 2 * way
        half = way if kind == 0 else 1 - way
        idx = (self.me[order[2]],) if p == 1 else ()
        out = lax.rem(self.me[a] - sign * (hop - 1) + n, n)
        got = lax.rem(self.me[a] - sign * hop + n, n)
        tail = (pl.ds(half * w, w),)
        b = self.buf[i]
        sems = (self.ag_send.at[i, p - 1, way, kind, hop - 1], self.ag_recv.at[i, p - 1, way, kind, hop - 1])
        dev = self.dev(**{a: sign})
        src, dst = b.at[idx + (out,) + tail], b.at[idx + (got,) + tail]
        return (src, src) + sems + (dev,), (dst, dst) + sems + (dev,)

    def gather_event(self, i, p, s):
        h = hops(STREAMS[i][0], p)
        ways = [(kind, way) for kind in (0, 1) for way in (0, 1)]
        if s == h:
            for kind, way in ways:
                self.remote(*self.gather_copy(i, p, way, kind, h - kind)[1]).wait_recv()
            return
        for kind, way in ways:
            if s == 0:
                self.send(*self.gather_copy(i, p, way, kind, 1)[0])
            elif s < h - kind:
                self.remote(*self.gather_copy(i, p, way, kind, s)[1]).wait_recv()
                self.send(*self.gather_copy(i, p, way, kind, s + 1)[0])

    def reduce_copy(self, i, p, way, kind, hop):
        order = STREAMS[i][0]
        w = SIZE[order[p - 1]] // 2
        half = way if kind == 0 else 1 - way
        at = (way, hop - 1, pl.ds(half * w, w))
        return (
            self.rs_out[i][p].at[at],
            self.rs_in[i][p].at[at],
            self.rs_send.at[i, p - 1, way, kind, hop - 1],
            self.rs_recv.at[i, p - 1, way, kind, hop - 1],
            self.dev(**{order[p]: 1 - 2 * way}),
        )

    def over(self, p, lo, size, body):
        if p == 2:
            for r in range(lo, lo + size):
                body((r,))
        else:
            body((pl.ds(lo, size),))

    def reduce_event(self, i, p, s):
        order = STREAMS[i][0]
        a = order[p]
        n, w, h = SIZE[a], SIZE[order[p - 1]] // 2, hops(order, p)
        part, out, got = self.part[i], self.rs_out[i][p], self.rs_in[i][p]
        base = (self.me[order[2]],) if p == 1 else ()
        ways = [(kind, way) for kind in (0, 1) for way in (0, 1)]
        if s == h:
            for kind, way in ways:
                self.remote(*self.reduce_copy(i, p, way, kind, h - kind)).wait_recv()
            mine = base + (self.me[a],)
            for half in (0, 1):
                far, near = (half, h - 1), (1 - half, h - 2)

                def add(r):
                    part[mine + r] = part[mine + r] + (got[far + r].astype(F32) + got[near + r].astype(F32))

                self.over(p, half * w, w, add)
            return
        for kind, way in ways:
            if s and s >= h - kind:
                continue
            if s:
                self.remote(*self.reduce_copy(i, p, way, kind, s)).wait_recv()
            half = way if kind == 0 else 1 - way
            d = h - kind - s
            idx = base + (lax.rem(self.me[a] + (1 - 2 * way) * d + n, n),)

            def put(r):
                v = part[idx + r]
                if s:
                    v = v + got[(way, s - 1) + r].astype(F32)
                out[(way, s) + r] = v.astype(BF16)

            self.over(p, half * w, w, put)
            self.send(*self.reduce_copy(i, p, way, kind, s + 1))

    def collect_copy(self, g, a, d):
        n = SIZE[a]
        to = lax.rem(self.me[a] + d, n)
        sems = self.last_sem[a]
        return self.remote(
            self.last_out[a].at[g, to],
            self.last_in[a].at[self.me[a], self.core],
            sems.at[0, g, d],
            sems.at[1, self.core, d],
            self.dev(core=g, **{a: d}),
        )

    def collect_send(self, g, a):
        col = WIDE[a][0]
        out = self.last_out[a]
        for i in range(NS):
            order, off, width = STREAMS[i]
            if order[0] == a:
                mine = self.part[i].at[self.me[order[2]], self.me[order[1]]]
                out[g, :, :, off - col : off - col + width] = mine[:, g * ROWS : (g + 1) * ROWS]

        for d in range(SIZE[a]):
            copy = self.collect_copy(g, a, d)
            if d:
                copy.start()
                self.sends.append(copy)
            else:

                @pl.when(self.core != g)
                def _():
                    copy.start()

                @pl.when(self.core == g)
                def _():
                    self.last_in[a][self.me[a], g] = out[g, self.me[a]]

    def collect_wait(self, g, a):
        n = SIZE[a]
        col, width = WIDE[a]
        sems = self.last_sem[a]
        buf = self.last_in[a]

        @pl.when(self.core == g)
        def _():
            for d in range(n):
                for c in (g, 1 - g):
                    if d or c != g:
                        slot = buf.at[lax.rem(self.me[a] - d + n, n), c]
                        self.remote(
                            slot, slot, sems.at[0, g, d], sems.at[1, c, d], self.dev(core=c, **{a: -d})
                        ).wait_recv()
            for c in (0, 1):
                v = buf[0, c]
                for e in range(1, n):
                    v = v + buf[e, c]
                self.gh[:, c * HALF + col : c * HALF + col + width] = v.astype(BF16)

        @pl.when(self.core != g)
        def _():
            self.collect_copy(g, a, 0).wait_send()

    def piece(self, i, y, zl):
        order, _, _ = STREAMS[i]
        return jnp.concatenate([self.buf[i][self.at(order, x, y, zh * ZL + zl)] for zh in range(ZH) for x in range(4)], axis=0)

    def at(self, order, x, y, z):
        c = {"x": x, "y": y, "z": z} | self.roles(x, y)
        return (c[order[2]], c[order[1]], c[order[0]])

    def hidden_block(self, j):
        y, zl = j // ZL, lax.rem(j, ZL)
        return jnp.concatenate([self.piece(i, y, zl) for i in range(NS)], axis=1)

    def gather(self):
        for i, (order, off, width) in enumerate(STREAMS):
            col = off - WIDE[order[0]][0]
            mine = self.buf[i].at[self.me[order[2]], self.me[order[1]]]
            for g in (0, 1):
                mine[:, g * ROWS : (g + 1) * ROWS] = self.first[order[0]][g, :, :, col : col + width]
            self.gather_event(i, 1, 0)
        for i in range(NS):
            self.gather_event(i, 1, 1)
        for i in LONG + SHORT:
            self.gather_event(i, 1, 2)
            self.gather_event(i, 2, 0)

        @pl.loop(0, NB)
        def _(j):
            self.weight_copies(j)[1].start()

        for streams, s in ((LONG, 1), (SHORT, 1), (LONG, 2), (LONG, 3), (SHORT, 2), (LONG, 4)):
            for i in streams:
                self.gather_event(i, 2, s)

    def drain(self, copies):
        for copy in copies:
            copy.wait_send()

    def reduce(self, meanwhile):
        before, self.sends = self.sends, []
        for i in LONG + SHORT:
            self.reduce_event(i, 2, 0)
        for streams, s in ((LONG, 1), (SHORT, 1), (LONG, 2), (LONG, 3)):
            next(meanwhile, None)
            if streams is SHORT:
                self.drain(before)
            for i in streams:
                self.reduce_event(i, 2, s)
        for i in SHORT:
            self.reduce_event(i, 2, 2)
            self.reduce_event(i, 1, 0)
        for i in LONG:
            self.reduce_event(i, 2, 4)
            self.reduce_event(i, 1, 0)
        for i in SHORT + LONG:
            self.reduce_event(i, 1, 1)
        for i in SHORT:
            self.reduce_event(i, 1, 2)
        for g in (0, 1):
            self.collect_send(g, "z")
        for i in LONG:
            self.reduce_event(i, 1, 2)
        before, self.sends = self.sends, []
        for g in (0, 1):
            self.collect_send(g, "y")
        self.drain(before)
        for g in (0, 1):
            self.collect_wait(g, "z")
        for g in (0, 1):
            self.collect_wait(g, "y")

    def loss_and_grads(self):
        self.wait_weight()
        acc = self.lg
        acc[...] = jnp.zeros_like(acc)

        @pl.loop(0, NB // BLOCKS)
        def _(b):
            js = [b * BLOCKS + e for e in range(BLOCKS)]
            acc[...] += lax.dot_general(
                jnp.concatenate([self.wv[j] for j in js], axis=1),
                jnp.concatenate([self.hidden_block(j) for j in js], axis=1),
                (((1,), (1,)), ((), ())),
                preferred_element_type=F32,
            )

        swap = (acc, self.lg_in, self.lg_sem.at[0], self.lg_sem.at[1], self.dev(core=1 - self.core))
        self.send(*swap)
        target, scale = self.tgt[...].reshape(1, -1), self.lw[...].reshape(1, -1)
        self.remote(*swap).wait_recv()
        logits = acc[...] + self.lg_in[...]
        self.lg_sum[...] = logits
        row = lax.broadcasted_iota(jnp.int32, logits.shape, 0)
        row = row + jnp.where(row < self.shard, self.vocab0, self.vocab0 + 15 * self.shard)
        hit = row == target
        top = jnp.max(logits, axis=0, keepdims=True)
        total = jnp.sum(jnp.exp(logits - top), axis=0, keepdims=True)
        picked = jnp.sum(jnp.where(hit, logits, 0.0), axis=0, keepdims=True)
        merged = self.stats(0, (top, total, picked), [(dx, dy, 0) for dx in range(4) for dy in range(4)])
        top, total, picked = self.stats(1, merged, [(0, 0, dz) for dz in range(8)])
        lse = top + jnp.log(total)
        self.loss[...] = (lse - picked).reshape(2 * NQ * ROWS)
        dl = scale * (jnp.exp(self.lg_sum[...] - lse) - (row == target).astype(F32))
        self.dlt[...] = dl.astype(BF16)
        self.dlr[...] = dl.T.astype(BF16)

        @pl.loop(0, NB, unroll=BLOCKS)
        def _(j):
            y, zl = j // ZL, lax.rem(j, ZL)
            o = jnp.dot(self.dlr[...], self.wv[j], preferred_element_type=F32)
            for i, (order, off, width) in enumerate(STREAMS):
                for zh in range(ZH):
                    for x in range(4):
                        q = (zh * 4 + x) * 2 * ROWS
                        self.part[i][self.at(order, x, y, zh * ZL + zl)] = o[q : q + 2 * ROWS, off : off + width]

    def stats(self, phase, mine, moves):
        buf = (self.st0, self.st1)[phase]
        own = self.me["x"] * 4 + self.me["y"] if phase == 0 else self.me["z"]
        sems = (self.st0_sem, self.st1_sem)[phase]
        pad = jnp.zeros((5, 256), F32)
        buf[own] = jnp.concatenate(mine + (pad,), axis=0)
        for e, (dx, dy, dz) in enumerate(moves):
            if e:
                self.send(buf.at[own], buf.at[own], sems.at[0, e], sems.at[1, e], self.dev(x=dx, y=dy, z=dz))
        for e, (dx, dy, dz) in enumerate(moves):
            if e:
                if phase == 0:
                    src = lax.rem(self.me["x"] - dx + 4, 4) * 4 + lax.rem(self.me["y"] - dy + 4, 4)
                else:
                    src = lax.rem(self.me["z"] - dz + 8, 8)
                self.remote(
                    buf.at[src], buf.at[src], sems.at[0, e], sems.at[1, e], self.dev(x=dx, y=dy, z=dz)
                ).wait_recv()
        tiles = [buf[e] for e in range(len(moves))]
        top = tiles[0][0:1]
        for t in tiles[1:]:
            top = jnp.maximum(top, t[0:1])
        total = picked = jnp.zeros_like(top)
        for t in tiles:
            total = total + t[1:2] * jnp.exp(t[0:1] - top)
            picked = picked + t[2:3]
        return (top, total, picked)

    def weight_copies(self, j):
        c, other = self.core, 1 - self.core
        rows = pl.ds(pl.multiple_of(c * self.shard, 16), self.shard)
        cols = lambda h: pl.ds(pl.multiple_of(j * FULL + h * HALF, HALF), HALF)
        theirs = pl.ds(pl.multiple_of(other * self.shard, 16), self.shard)
        local = pltpu.make_async_copy(self.w.at[:, cols(c)], self.wv.at[j, rows], self.w_sem.at[0, j])
        out = self.remote(
            self.w.at[:, cols(other)], self.wv.at[j, rows], self.w_sem.at[1, j], self.w_sem.at[2, j], self.dev(core=other)
        )
        arrive = self.remote(
            self.w.at[:, cols(other)], self.wv.at[j, theirs], self.w_sem.at[1, j], self.w_sem.at[2, j], self.dev(core=other)
        )
        return local, out, arrive

    def wait_weight(self):
        @pl.loop(0, NB)
        def _(j):
            local, out, arrive = self.weight_copies(j)
            local.wait()
            out.wait_send()
            arrive.wait_recv()

    def grad_copies(self, j):
        c, other = self.core, 1 - self.core
        cols = lambda h: pl.ds(pl.multiple_of(j * FULL + h * HALF, HALF), HALF)
        src = lambda h: self.gwb.at[j, pl.ds(pl.multiple_of(h * self.shard, 16), self.shard)]
        local = pltpu.make_async_copy(src(c), self.gw.at[:, cols(c)], self.g_sem.at[0, j])
        dev = self.dev(core=other)
        out = self.remote(src(other), self.gw.at[:, cols(c)], self.g_sem.at[1, j], self.g_sem.at[2, j], dev)
        arrive = self.remote(src(other), self.gw.at[:, cols(other)], self.g_sem.at[1, j], self.g_sem.at[2, j], dev)
        return local, out, arrive

    def grad_weight(self, lo, hi):
        @pl.loop(lo, hi, unroll=BLOCKS)
        def _(j):
            o = jnp.dot(self.dlt[...], self.hidden_block(j), preferred_element_type=F32)
            self.gwb[j] = o.astype(BF16)
            local, out, _ = self.grad_copies(j)
            local.start()
            out.start()

    def grad_quarters(self):
        for q in range(4):
            self.grad_weight(q * (NB // 4), (q + 1) * (NB // 4))
            yield

    def run(self):
        other = 1 - self.core
        barrier = pltpu.get_barrier_semaphore()
        peers = [dict(x=dx, y=dy) for dx in range(4) for dy in range(4) if dx or dy]
        peers += [dict(z=dz) for dz in range(1, 8)]
        peers += [dict(core=other, z=dz) for dz in range(8)]
        peers += [dict(core=other, y=dy) for dy in range(1, 4)]
        for d in peers:
            pl.semaphore_signal(barrier, inc=1, device_id=self.dev(**d), device_id_type=MESH)
        for a in ("z", "y"):
            self.spread_copy(a, 0, 0)[0].start()

        @pl.loop(0, NB)
        def _(j):
            self.weight_copies(j)[0].start()

        pl.semaphore_wait(barrier, len(peers))
        self.spread()
        self.spread_wait()
        self.gather()
        self.loss_and_grads()
        self.reduce(self.grad_quarters())

        @pl.loop(0, NB)
        def _(j):
            local, out, arrive = self.grad_copies(j)
            local.wait()
            out.wait_send()
            arrive.wait_recv()

        self.drain(self.sends)


def scratch(shard):
    dma = pltpu.SemaphoreType.DMA
    rows = 2 * shard
    out = {
        "wv": pltpu.VMEM((NB, rows, HALF), BF16),
        "lg": pltpu.VMEM((rows, 256), F32),
        "lg_in": pltpu.VMEM((rows, 256), F32),
        "lg_sum": pltpu.VMEM((rows, 256), F32),
        "st0": pltpu.VMEM((16, 8, 256), F32),
        "st1": pltpu.VMEM((8, 8, 256), F32),
        "dlt": pltpu.VMEM((rows, 256), BF16),
        "dlr": pltpu.VMEM((256, rows), BF16),
        "gwb": pltpu.VMEM((NB, rows, HALF), BF16),
        "ag_send": dma((NS, 2, 2, 2, 4)),
        "ag_recv": dma((NS, 2, 2, 2, 4)),
        "rs_send": dma((NS, 2, 2, 2, 4)),
        "rs_recv": dma((NS, 2, 2, 2, 4)),
        "lg_sem": dma((2,)),
        "st0_sem": dma((2, 16)),
        "st1_sem": dma((2, 8)),
        "w_sem": dma((3, NB)),
        "g_sem": dma((3, NB)),
    }
    for a in ("z", "y"):
        n, width = SIZE[a], WIDE[a][1]
        out[f"first{a}"] = pltpu.VMEM((2, n, ROWS, width), BF16)
        out[f"first_sem{a}"] = dma((2, 2, n))
        out[f"last_out{a}"] = pltpu.VMEM((2, n, ROWS, width), F32)
        out[f"last_in{a}"] = pltpu.VMEM((n, 2, ROWS, width), F32)
        out[f"last_sem{a}"] = dma((2, 2, n))
    for i, (order, _, width) in enumerate(STREAMS):
        l, m, f = lead(order)
        out[f"buf{i}"] = pltpu.VMEM((l, m, f, 2 * ROWS, width), BF16)
        out[f"part{i}"] = pltpu.VMEM((l, m, f, 2 * ROWS, width), F32)
        chunk = {2: (m, f, 2 * ROWS, width), 1: (f, 2 * ROWS, width)}
        for p in (1, 2):
            shape = (2, hops(order, p)) + chunk[p]
            out[f"rs_out{i}{p}"] = pltpu.VMEM(shape, BF16)
            out[f"rs_in{i}{p}"] = pltpu.VMEM(shape, BF16)
    return out


def on_device(hidden, head_weight, targets, loss_weight):
    shard, width = head_weight.shape
    spaces = scratch(shard)

    def body(hid, w, tgt, lw, loss, gw, gh, *refs):
        named = dict(zip(spaces, refs))
        args = dict(hid=hid, w=w, tgt=tgt, lw=lw, loss=loss, gw=gw, gh=gh)
        for kind in ("buf", "part"):
            args[kind] = [named.pop(f"{kind}{i}") for i in range(NS)]
        for kind in ("rs_out", "rs_in"):
            args[kind] = [{p: named.pop(f"{kind}{i}{p}") for p in (1, 2)} for i in range(NS)]
        for kind in ("first", "first_sem", "last_out", "last_in", "last_sem"):
            args[kind] = {a: named.pop(f"{kind}{a}") for a in ("z", "y")}
        args.update(named)
        Kernel(shard, args).run()

    vmem, hbm = pl.BlockSpec(memory_space=pltpu.VMEM), pl.BlockSpec(memory_space=pl.ANY)
    loss, gw, gh = pl.pallas_call(
        body,
        out_shape=(
            jax.ShapeDtypeStruct(loss_weight.shape, F32),
            jax.ShapeDtypeStruct((shard, width), BF16),
            jax.ShapeDtypeStruct(hidden.shape, BF16),
        ),
        in_specs=[hbm, hbm, vmem, vmem],
        out_specs=(vmem, hbm, vmem),
        scratch_shapes=list(spaces.values()),
        compiler_params=pltpu.CompilerParams(
            collective_id=0, has_side_effects=True, vmem_limit_bytes=56 * 1024 * 1024
        ),
        cost_estimate=pl.CostEstimate(
            flops=6 * shard * width * 256, bytes_accessed=4 * shard * width, transcendentals=2 * shard * 512
        ),
    )(hidden, head_weight, targets, loss_weight)
    return (loss, gw, gh)


def solution(mesh):
    in_specs = (P("section", "tensor"), P(("section", "tensor"), None), P(), P())
    out_specs = (P(), P(("section", "tensor"), None), P("section", "tensor"))
    return jax.shard_map(
        on_device, mesh=mesh, in_specs=in_specs, out_specs=out_specs, check_vma=False
    )
```

```python
import math

import jax
import jax.numpy as jnp
from jax import lax
from jax.experimental import pallas as pl
from jax.experimental.pallas import tpu as pltpu
from jax.sharding import PartitionSpec as P

MESH = pl.DeviceIdType.MESH
F32, BF16 = jnp.float32, jnp.bfloat16
SIZE = {"x": 4, "y": 4, "z": 8, "a": 4, "b": 4}
ZH, ZL = 2, 4
NB = SIZE["y"] * ZL
NQ = ZH * SIZE["x"]
ROWS = 16
FULL, HALF = 1024, 512
STREAMS = (
    (("z", "b", "a"), 0, 256),
    (("z", "a", "b"), 256, 128),
    (("y", "x", "z"), 384, 128),
)
NS = len(STREAMS)
WIDE = {"z": (0, 384), "y": (384, 128)}
LONG = [i for i in range(NS) if STREAMS[i][0][2] == "z"]
SHORT = [i for i in range(NS) if i not in LONG]
BLOCKS = 4


def flat(ref, idx, count):
    dims = ref.shape[:-1]
    start, rows = 0, math.prod(dims[len(idx) :])
    for e, n in zip(idx, dims):
        start = start * n + e
    start = pl.multiple_of(start * rows, 32)
    return ref.reshape(math.prod(dims), ref.shape[-1]).at[pl.ds(start, count * rows)]


def lead(order):
    f, m, l = (SIZE[a] for a in order)
    return (l, m, f)


def hops(order, p):
    return SIZE[order[p]] // 2


class Kernel:
    def __init__(self, shard, refs):
        self.shard = shard
        self.__dict__.update(refs)
        sec, ten = lax.axis_index("section"), lax.axis_index("tensor")
        self.core = lax.rem(sec, 2)
        z = (sec // 8) * 4 + lax.rem(ten, 4)
        x, y = lax.rem(sec // 2, 4), ten // 4
        self.me = {"x": x, "y": y, "z": z} | self.roles(x, y)
        self.vocab0 = ((sec - self.core) * 16 + ten) * shard
        self.sends = []

    def roles(self, x, y):
        return {"a": jnp.where(self.core == 0, y, x), "b": jnp.where(self.core == 0, x, y)}

    def dev(self, core=None, **move):
        c = dict(self.me)
        for a, d in move.items():
            c[a] = lax.rem(c[a] + d + SIZE[a], SIZE[a])
            if a in ("a", "b"):
                first = self.core == (0 if a == "b" else 1)
                c["x"], c["y"] = jnp.where(first, c[a], c["x"]), jnp.where(first, c["y"], c[a])
        core = self.core if core is None else core
        return ((c["z"] // 4) * 8 + c["x"] * 2 + core, c["y"] * 4 + lax.rem(c["z"], 4))

    def remote(self, src, dst, ssem, rsem, device):
        return pltpu.make_async_remote_copy(
            src_ref=src, dst_ref=dst, send_sem=ssem, recv_sem=rsem, device_id=device, device_id_type=MESH
        )

    def send(self, *args):
        copy = self.remote(*args)
        copy.start()
        self.sends.append(copy)
        return copy

    def spread_copy(self, a, r, d):
        n = SIZE[a]
        col, width = WIDE[a]
        other = 1 - self.core
        to_core = other if r else self.core
        src = self.hid.at[:, pl.ds(pl.multiple_of(to_core * HALF + col, 128), width)]
        buf, sem = self.first[a], self.first_sem[a]
        if r == 0 and d == 0:
            return pltpu.make_async_copy(src, buf.at[self.core, self.me[a]], sem.at[1, 0, 0]), None
        dev = self.dev(core=to_core, **{a: d})
        sems = (sem.at[0, r, d], sem.at[1, r, d], dev)
        got = buf.at[to_core, lax.rem(self.me[a] - d + n, n)]
        return self.remote(src, buf.at[self.core, self.me[a]], *sems), self.remote(src, got, *sems)

    def spread(self):
        for a in ("z", "y"):
            for d in range(SIZE[a]):
                for r in (0, 1):
                    if d or r:
                        copy, _ = self.spread_copy(a, r, d)
                        copy.start()
                        self.sends.append(copy)

    def spread_wait(self):
        for a in ("z", "y"):
            for d in range(SIZE[a]):
                for r in (0, 1):
                    local, got = self.spread_copy(a, r, d)
                    if got is None:
                        local.wait()
                    else:
                        got.wait_recv()

    def gather_copy(self, i, p, way, kind, hop):
        order = STREAMS[i][0]
        a = order[p]
        n, w = SIZE[a], SIZE[order[p - 1]] // 2
        sign = 1 - 2 * way
        half = way if kind == 0 else 1 - way
        idx = (self.me[order[2]],) if p == 1 else ()
        out = lax.rem(self.me[a] - sign * (hop - 1) + n, n)
        got = lax.rem(self.me[a] - sign * hop + n, n)
        at = half * w
        sems = (self.ag_send.at[i, p - 1, way, kind, hop - 1], self.ag_recv.at[i, p - 1, way, kind, hop - 1])
        dev = self.dev(**{a: sign})
        src, dst = (flat(self.buf[i], idx + (e, at), w) for e in (out, got))
        return (src, src) + sems + (dev,), (dst, dst) + sems + (dev,)

    def gather_event(self, i, p, s):
        h = hops(STREAMS[i][0], p)
        ways = [(kind, way) for kind in (0, 1) for way in (0, 1)]
        if s == h:
            for kind, way in ways:
                self.remote(*self.gather_copy(i, p, way, kind, h - kind)[1]).wait_recv()
            return
        for kind, way in ways:
            if s == 0:
                self.send(*self.gather_copy(i, p, way, kind, 1)[0])
            elif s < h - kind:
                self.remote(*self.gather_copy(i, p, way, kind, s)[1]).wait_recv()
                self.send(*self.gather_copy(i, p, way, kind, s + 1)[0])

    def reduce_copy(self, i, p, way, kind, hop):
        order = STREAMS[i][0]
        w = SIZE[order[p - 1]] // 2
        half = way if kind == 0 else 1 - way
        at = (way, hop - 1, half * w)
        return (
            flat(self.rs_out[i][p], at, w),
            flat(self.rs_in[i][p], at, w),
            self.rs_send.at[i, p - 1, way, kind, hop - 1],
            self.rs_recv.at[i, p - 1, way, kind, hop - 1],
            self.dev(**{order[p]: 1 - 2 * way}),
        )

    def over(self, p, lo, size, body):
        if p == 2:
            for r in range(lo, lo + size):
                body((r,))
        else:
            body((pl.ds(lo, size),))

    def reduce_event(self, i, p, s):
        order = STREAMS[i][0]
        a = order[p]
        n, w, h = SIZE[a], SIZE[order[p - 1]] // 2, hops(order, p)
        part, out, got = self.part[i], self.rs_out[i][p], self.rs_in[i][p]
        base = (self.me[order[2]],) if p == 1 else ()
        ways = [(kind, way) for kind in (0, 1) for way in (0, 1)]
        if s == h:
            for kind, way in ways:
                self.remote(*self.reduce_copy(i, p, way, kind, h - kind)).wait_recv()
            mine = base + (self.me[a],)
            for half in (0, 1):
                far, near = (half, h - 1), (1 - half, h - 2)

                def add(r):
                    part[mine + r] = part[mine + r] + (got[far + r].astype(F32) + got[near + r].astype(F32))

                self.over(p, half * w, w, add)
            return
        for kind, way in ways:
            if s and s >= h - kind:
                continue
            if s:
                self.remote(*self.reduce_copy(i, p, way, kind, s)).wait_recv()
            half = way if kind == 0 else 1 - way
            d = h - kind - s
            idx = base + (lax.rem(self.me[a] + (1 - 2 * way) * d + n, n),)

            def put(r):
                v = part[idx + r]
                if s:
                    v = v + got[(way, s - 1) + r].astype(F32)
                out[(way, s) + r] = v.astype(BF16)

            self.over(p, half * w, w, put)
            self.send(*self.reduce_copy(i, p, way, kind, s + 1))

    def collect_copy(self, g, a, d):
        n = SIZE[a]
        to = lax.rem(self.me[a] + d, n)
        sems = self.last_sem[a]
        return self.remote(
            self.last_out[a].at[g, to],
            self.last_in[a].at[self.me[a], self.core],
            sems.at[0, g, d],
            sems.at[1, self.core, d],
            self.dev(core=g, **{a: d}),
        )

    def collect_send(self, g, a):
        col = WIDE[a][0]
        out = self.last_out[a]
        for i in range(NS):
            order, off, width = STREAMS[i]
            if order[0] == a:
                mine = self.part[i].at[self.me[order[2]], self.me[order[1]]]
                out[g, :, :, off - col : off - col + width] = mine[:, g * ROWS : (g + 1) * ROWS]

        for d in range(SIZE[a]):
            copy = self.collect_copy(g, a, d)
            if d:
                copy.start()
                self.sends.append(copy)
            else:

                @pl.when(self.core != g)
                def _():
                    copy.start()

                @pl.when(self.core == g)
                def _():
                    self.last_in[a][self.me[a], g] = out[g, self.me[a]]

    def collect_wait(self, g, a):
        n = SIZE[a]
        col, width = WIDE[a]
        sems = self.last_sem[a]
        buf = self.last_in[a]

        @pl.when(self.core == g)
        def _():
            for d in range(n):
                for c in (g, 1 - g):
                    if d or c != g:
                        slot = buf.at[lax.rem(self.me[a] - d + n, n), c]
                        self.remote(
                            slot, slot, sems.at[0, g, d], sems.at[1, c, d], self.dev(core=c, **{a: -d})
                        ).wait_recv()
            for c in (0, 1):
                v = buf[0, c]
                for e in range(1, n):
                    v = v + buf[e, c]
                self.gh[:, c * HALF + col : c * HALF + col + width] = v.astype(BF16)

        @pl.when(self.core != g)
        def _():
            self.collect_copy(g, a, 0).wait_send()

    def piece(self, i, y, zl):
        order, _, _ = STREAMS[i]
        return jnp.concatenate([self.buf[i][self.at(order, x, y, zh * ZL + zl)] for zh in range(ZH) for x in range(4)], axis=0)

    def at(self, order, x, y, z):
        c = {"x": x, "y": y, "z": z} | self.roles(x, y)
        return (c[order[2]], c[order[1]], c[order[0]])

    def hidden_block(self, j):
        y, zl = j // ZL, lax.rem(j, ZL)
        return jnp.concatenate([self.piece(i, y, zl) for i in range(NS)], axis=1)

    def gather(self):
        for i, (order, off, width) in enumerate(STREAMS):
            col = off - WIDE[order[0]][0]
            mine = self.buf[i].at[self.me[order[2]], self.me[order[1]]]
            for g in (0, 1):
                mine[:, g * ROWS : (g + 1) * ROWS] = self.first[order[0]][g, :, :, col : col + width]
            self.gather_event(i, 1, 0)
        for i in range(NS):
            self.gather_event(i, 1, 1)
        for i in LONG + SHORT:
            self.gather_event(i, 1, 2)
            self.gather_event(i, 2, 0)

        @pl.loop(0, NB)
        def _(j):
            self.weight_copies(j)[1].start()

        for streams, s in ((LONG, 1), (SHORT, 1), (LONG, 2), (LONG, 3), (SHORT, 2), (LONG, 4)):
            for i in streams:
                self.gather_event(i, 2, s)

    def drain(self, copies):
        for copy in copies:
            copy.wait_send()

    def reduce(self, meanwhile):
        before, self.sends = self.sends, []
        for i in LONG + SHORT:
            self.reduce_event(i, 2, 0)
        for streams, s in ((LONG, 1), (SHORT, 1), (LONG, 2), (LONG, 3)):
            next(meanwhile, None)
            if streams is SHORT:
                self.drain(before)
            for i in streams:
                self.reduce_event(i, 2, s)
        for i in SHORT:
            self.reduce_event(i, 2, 2)
            self.reduce_event(i, 1, 0)
        for i in LONG:
            self.reduce_event(i, 2, 4)
            self.reduce_event(i, 1, 0)
        for i in SHORT + LONG:
            self.reduce_event(i, 1, 1)
        for i in SHORT:
            self.reduce_event(i, 1, 2)
        for g in (0, 1):
            self.collect_send(g, "z")
        for i in LONG:
            self.reduce_event(i, 1, 2)
        before, self.sends = self.sends, []
        for g in (0, 1):
            self.collect_send(g, "y")
        self.drain(before)
        for g in (0, 1):
            self.collect_wait(g, "z")
        for g in (0, 1):
            self.collect_wait(g, "y")

    def loss_and_grads(self):
        self.wait_weight()
        acc = self.lg
        acc[...] = jnp.zeros_like(acc)

        @pl.loop(0, NB // BLOCKS)
        def _(b):
            js = [b * BLOCKS + e for e in range(BLOCKS)]
            acc[...] += lax.dot_general(
                jnp.concatenate([self.wv[j] for j in js], axis=1),
                jnp.concatenate([self.hidden_block(j) for j in js], axis=1),
                (((1,), (1,)), ((), ())),
                preferred_element_type=F32,
            )

        swap = (acc, self.lg_in, self.lg_sem.at[0], self.lg_sem.at[1], self.dev(core=1 - self.core))
        self.send(*swap)
        target, scale = self.tgt[...].reshape(1, -1), self.lw[...].reshape(1, -1)
        self.remote(*swap).wait_recv()
        logits = acc[...] + self.lg_in[...]
        self.lg_sum[...] = logits
        row = lax.broadcasted_iota(jnp.int32, logits.shape, 0)
        row = row + jnp.where(row < self.shard, self.vocab0, self.vocab0 + 15 * self.shard)
        hit = row == target
        top = jnp.max(logits, axis=0, keepdims=True)
        total = jnp.sum(jnp.exp(logits - top), axis=0, keepdims=True)
        picked = jnp.sum(jnp.where(hit, logits, 0.0), axis=0, keepdims=True)
        merged = self.stats(0, (top, total, picked), [(dx, dy, 0) for dx in range(4) for dy in range(4)])
        top, total, picked = self.stats(1, merged, [(0, 0, dz) for dz in range(8)])
        lse = top + jnp.log(total)
        self.loss[...] = (lse - picked).reshape(2 * NQ * ROWS)
        dl = scale * (jnp.exp(self.lg_sum[...] - lse) - (row == target).astype(F32))
        self.dlt[...] = dl.astype(BF16)
        self.dlr[...] = dl.T.astype(BF16)

        @pl.loop(0, NB, unroll=BLOCKS)
        def _(j):
            y, zl = j // ZL, lax.rem(j, ZL)
            o = jnp.dot(self.dlr[...], self.wv[j], preferred_element_type=F32)
            for i, (order, off, width) in enumerate(STREAMS):
                for zh in range(ZH):
                    for x in range(4):
                        q = (zh * 4 + x) * 2 * ROWS
                        self.part[i][self.at(order, x, y, zh * ZL + zl)] = o[q : q + 2 * ROWS, off : off + width]

    def stats(self, phase, mine, moves):
        buf = (self.st0, self.st1)[phase]
        own = self.me["x"] * 4 + self.me["y"] if phase == 0 else self.me["z"]
        sems = (self.st0_sem, self.st1_sem)[phase]
        pad = jnp.zeros((5, 256), F32)
        buf[own] = jnp.concatenate(mine + (pad,), axis=0)
        for e, (dx, dy, dz) in enumerate(moves):
            if e:
                self.send(buf.at[own], buf.at[own], sems.at[0, e], sems.at[1, e], self.dev(x=dx, y=dy, z=dz))
        for e, (dx, dy, dz) in enumerate(moves):
            if e:
                if phase == 0:
                    src = lax.rem(self.me["x"] - dx + 4, 4) * 4 + lax.rem(self.me["y"] - dy + 4, 4)
                else:
                    src = lax.rem(self.me["z"] - dz + 8, 8)
                self.remote(
                    buf.at[src], buf.at[src], sems.at[0, e], sems.at[1, e], self.dev(x=dx, y=dy, z=dz)
                ).wait_recv()
        tiles = [buf[e] for e in range(len(moves))]
        top = tiles[0][0:1]
        for t in tiles[1:]:
            top = jnp.maximum(top, t[0:1])
        total = picked = jnp.zeros_like(top)
        for t in tiles:
            total = total + t[1:2] * jnp.exp(t[0:1] - top)
            picked = picked + t[2:3]
        return (top, total, picked)

    def weight_copies(self, j):
        c, other = self.core, 1 - self.core
        rows = pl.ds(pl.multiple_of(c * self.shard, 16), self.shard)
        cols = lambda h: pl.ds(pl.multiple_of(j * FULL + h * HALF, HALF), HALF)
        theirs = pl.ds(pl.multiple_of(other * self.shard, 16), self.shard)
        local = pltpu.make_async_copy(self.w.at[:, cols(c)], self.wv.at[j, rows], self.w_sem.at[0, j])
        out = self.remote(
            self.w.at[:, cols(other)], self.wv.at[j, rows], self.w_sem.at[1, j], self.w_sem.at[2, j], self.dev(core=other)
        )
        arrive = self.remote(
            self.w.at[:, cols(other)], self.wv.at[j, theirs], self.w_sem.at[1, j], self.w_sem.at[2, j], self.dev(core=other)
        )
        return local, out, arrive

    def wait_weight(self):
        @pl.loop(0, NB)
        def _(j):
            local, out, arrive = self.weight_copies(j)
            local.wait()
            out.wait_send()
            arrive.wait_recv()

    def grad_copies(self, j):
        c, other = self.core, 1 - self.core
        cols = lambda h: pl.ds(pl.multiple_of(j * FULL + h * HALF, HALF), HALF)
        src = lambda h: self.gwb.at[j, pl.ds(pl.multiple_of(h * self.shard, 16), self.shard)]
        local = pltpu.make_async_copy(src(c), self.gw.at[:, cols(c)], self.g_sem.at[0, j])
        dev = self.dev(core=other)
        out = self.remote(src(other), self.gw.at[:, cols(c)], self.g_sem.at[1, j], self.g_sem.at[2, j], dev)
        arrive = self.remote(src(other), self.gw.at[:, cols(other)], self.g_sem.at[1, j], self.g_sem.at[2, j], dev)
        return local, out, arrive

    def grad_weight(self, lo, hi):
        @pl.loop(lo, hi, unroll=BLOCKS)
        def _(j):
            o = jnp.dot(self.dlt[...], self.hidden_block(j), preferred_element_type=F32)
            self.gwb[j] = o.astype(BF16)
            local, out, _ = self.grad_copies(j)
            local.start()
            out.start()

    def grad_quarters(self):
        for q in range(4):
            self.grad_weight(q * (NB // 4), (q + 1) * (NB // 4))
            yield

    def run(self):
        other = 1 - self.core
        barrier = pltpu.get_barrier_semaphore()
        peers = [dict(x=dx, y=dy) for dx in range(4) for dy in range(4) if dx or dy]
        peers += [dict(z=dz) for dz in range(1, 8)]
        peers += [dict(core=other, z=dz) for dz in range(8)]
        peers += [dict(core=other, y=dy) for dy in range(1, 4)]
        for d in peers:
            pl.semaphore_signal(barrier, inc=1, device_id=self.dev(**d), device_id_type=MESH)
        for a in ("z", "y"):
            self.spread_copy(a, 0, 0)[0].start()

        @pl.loop(0, NB)
        def _(j):
            self.weight_copies(j)[0].start()

        pl.semaphore_wait(barrier, len(peers))
        self.spread()
        self.spread_wait()
        self.gather()
        self.loss_and_grads()
        self.reduce(self.grad_quarters())

        @pl.loop(0, NB)
        def _(j):
            local, out, arrive = self.grad_copies(j)
            local.wait()
            out.wait_send()
            arrive.wait_recv()

        self.drain(self.sends)


def scratch(shard):
    dma = pltpu.SemaphoreType.DMA
    rows = 2 * shard
    out = {
        "wv": pltpu.VMEM((NB, rows, HALF), BF16),
        "lg": pltpu.VMEM((rows, 256), F32),
        "lg_in": pltpu.VMEM((rows, 256), F32),
        "lg_sum": pltpu.VMEM((rows, 256), F32),
        "st0": pltpu.VMEM((16, 8, 256), F32),
        "st1": pltpu.VMEM((8, 8, 256), F32),
        "dlt": pltpu.VMEM((rows, 256), BF16),
        "dlr": pltpu.VMEM((256, rows), BF16),
        "gwb": pltpu.VMEM((NB, rows, HALF), BF16),
        "ag_send": dma((NS, 2, 2, 2, 4)),
        "ag_recv": dma((NS, 2, 2, 2, 4)),
        "rs_send": dma((NS, 2, 2, 2, 4)),
        "rs_recv": dma((NS, 2, 2, 2, 4)),
        "lg_sem": dma((2,)),
        "st0_sem": dma((2, 16)),
        "st1_sem": dma((2, 8)),
        "w_sem": dma((3, NB)),
        "g_sem": dma((3, NB)),
    }
    for a in ("z", "y"):
        n, width = SIZE[a], WIDE[a][1]
        out[f"first{a}"] = pltpu.VMEM((2, n, ROWS, width), BF16)
        out[f"first_sem{a}"] = dma((2, 2, n))
        out[f"last_out{a}"] = pltpu.VMEM((2, n, ROWS, width), F32)
        out[f"last_in{a}"] = pltpu.VMEM((n, 2, ROWS, width), F32)
        out[f"last_sem{a}"] = dma((2, 2, n))
    for i, (order, _, width) in enumerate(STREAMS):
        l, m, f = lead(order)
        out[f"buf{i}"] = pltpu.VMEM((l, m, f, 2 * ROWS, width), BF16)
        out[f"part{i}"] = pltpu.VMEM((l, m, f, 2 * ROWS, width), F32)
        chunk = {2: (m, f, 2 * ROWS, width), 1: (f, 2 * ROWS, width)}
        for p in (1, 2):
            shape = (2, hops(order, p)) + chunk[p]
            out[f"rs_out{i}{p}"] = pltpu.VMEM(shape, BF16)
            out[f"rs_in{i}{p}"] = pltpu.VMEM(shape, BF16)
    return out


def on_device(hidden, head_weight, targets, loss_weight):
    shard, width = head_weight.shape
    spaces = scratch(shard)

    def body(hid, w, tgt, lw, loss, gw, gh, *refs):
        named = dict(zip(spaces, refs))
        args = dict(hid=hid, w=w, tgt=tgt, lw=lw, loss=loss, gw=gw, gh=gh)
        for kind in ("buf", "part"):
            args[kind] = [named.pop(f"{kind}{i}") for i in range(NS)]
        for kind in ("rs_out", "rs_in"):
            args[kind] = [{p: named.pop(f"{kind}{i}{p}") for p in (1, 2)} for i in range(NS)]
        for kind in ("first", "first_sem", "last_out", "last_in", "last_sem"):
            args[kind] = {a: named.pop(f"{kind}{a}") for a in ("z", "y")}
        args.update(named)
        Kernel(shard, args).run()

    vmem, hbm = pl.BlockSpec(memory_space=pltpu.VMEM), pl.BlockSpec(memory_space=pl.ANY)
    loss, gw, gh = pl.pallas_call(
        body,
        out_shape=(
            pltpu.VMEM(loss_weight.shape, F32),
            pltpu.VMEM((shard, width), BF16),
            pltpu.VMEM(hidden.shape, BF16),
        ),
        in_specs=[hbm, hbm, vmem, vmem],
        out_specs=(vmem, vmem, vmem),
        scratch_shapes=list(spaces.values()),
        compiler_params=pltpu.CompilerParams(
            collective_id=0, has_side_effects=True, vmem_limit_bytes=56 * 1024 * 1024
        ),
        cost_estimate=pl.CostEstimate(
            flops=6 * shard * width * 256, bytes_accessed=4 * shard * width, transcendentals=2 * shard * 512
        ),
    )(hidden, head_weight, targets, loss_weight)
    return (loss, gw, gh)


def solution(mesh):
    in_specs = (P("section", "tensor"), P(("section", "tensor"), None), P(), P())
    out_specs = (P(), P(("section", "tensor"), None), P("section", "tensor"))
    return jax.shard_map(
        on_device, mesh=mesh, in_specs=in_specs, out_specs=out_specs, check_vma=False
    )
```

```python
import jax
import jax.numpy as jnp
from jax import lax
from jax.experimental import pallas as pl
from jax.experimental.pallas import tpu as pltpu
from jax.sharding import PartitionSpec as P

MESH = pl.DeviceIdType.MESH
F32, BF16 = jnp.float32, jnp.bfloat16
SIZE = {"x": 4, "y": 4, "z": 8, "a": 4, "b": 4}
ZH, ZL = 2, 4
NB = SIZE["y"] * ZL
NQ = ZH * SIZE["x"]
ROWS = 16
FULL, HALF = 1024, 512
STREAMS = (
    (("z", "b", "a"), 0, 256),
    (("z", "a", "b"), 256, 128),
    (("y", "x", "z"), 384, 128),
)
NS = len(STREAMS)
WIDE = {"z": (0, 384), "y": (384, 128)}
LONG = [i for i in range(NS) if STREAMS[i][0][2] == "z"]
SHORT = [i for i in range(NS) if i not in LONG]
BLOCKS = 4


def lead(order):
    f, m, l = (SIZE[a] for a in order)
    return (l, m, f)


def hops(order, p):
    return SIZE[order[p]] // 2


class Kernel:
    def __init__(self, shard, refs):
        self.shard = shard
        self.__dict__.update(refs)
        sec, ten = lax.axis_index("section"), lax.axis_index("tensor")
        self.core = lax.rem(sec, 2)
        z = (sec // 8) * 4 + lax.rem(ten, 4)
        x, y = lax.rem(sec // 2, 4), ten // 4
        self.me = {"x": x, "y": y, "z": z} | self.roles(x, y)
        self.vocab0 = ((sec - self.core) * 16 + ten) * shard
        self.sends = []

    def roles(self, x, y):
        return {"a": jnp.where(self.core == 0, y, x), "b": jnp.where(self.core == 0, x, y)}

    def dev(self, core=None, **move):
        c = dict(self.me)
        for a, d in move.items():
            c[a] = lax.rem(c[a] + d + SIZE[a], SIZE[a])
            if a in ("a", "b"):
                first = self.core == (0 if a == "b" else 1)
                c["x"], c["y"] = jnp.where(first, c[a], c["x"]), jnp.where(first, c["y"], c[a])
        core = self.core if core is None else core
        return ((c["z"] // 4) * 8 + c["x"] * 2 + core, c["y"] * 4 + lax.rem(c["z"], 4))

    def remote(self, src, dst, ssem, rsem, device):
        return pltpu.make_async_remote_copy(
            src_ref=src, dst_ref=dst, send_sem=ssem, recv_sem=rsem, device_id=device, device_id_type=MESH
        )

    def send(self, *args):
        copy = self.remote(*args)
        copy.start()
        self.sends.append(copy)
        return copy

    def spread_copy(self, a, r, d):
        n = SIZE[a]
        col, width = WIDE[a]
        other = 1 - self.core
        to_core = other if r else self.core
        src = self.hid.at[:, pl.ds(pl.multiple_of(to_core * HALF + col, 128), width)]
        buf, sem = self.first[a], self.first_sem[a]
        if r == 0 and d == 0:
            return pltpu.make_async_copy(src, buf.at[self.core, self.me[a]], sem.at[1, 0, 0]), None
        dev = self.dev(core=to_core, **{a: d})
        sems = (sem.at[0, r, d], sem.at[1, r, d], dev)
        got = buf.at[to_core, lax.rem(self.me[a] - d + n, n)]
        return self.remote(src, buf.at[self.core, self.me[a]], *sems), self.remote(src, got, *sems)

    def spread(self):
        for a in ("z", "y"):
            for d in range(SIZE[a]):
                for r in (0, 1):
                    if d or r:
                        copy, _ = self.spread_copy(a, r, d)
                        copy.start()
                        self.sends.append(copy)

    def spread_wait(self):
        for a in ("z", "y"):
            for d in range(SIZE[a]):
                for r in (0, 1):
                    local, got = self.spread_copy(a, r, d)
                    if got is None:
                        local.wait()
                    else:
                        got.wait_recv()

    def gather_copy(self, i, p, g, way, kind, hop):
        order = STREAMS[i][0]
        a = order[p]
        n, w = SIZE[a], SIZE[order[p - 1]] // 2
        sign = 1 - 2 * way
        half = way if kind == 0 else 1 - way
        tail = pl.ds(half * w, w)
        out = lax.rem(self.me[a] - sign * (hop - 1) + n, n)
        got = lax.rem(self.me[a] - sign * hop + n, n)
        at = (i, 0 if p == 1 else 1 + g, way, kind, hop - 1)
        sems = (self.ag_send.at[at], self.ag_recv.at[at])
        dev = self.dev(**{a: sign})
        if p == 1:
            src, dst = (self.buf[i].at[:, self.me[order[2]], e, tail] for e in (out, got))
        else:
            src, dst = (self.buf[i].at[g, e, tail] for e in (out, got))
        return (src, src) + sems + (dev,), (dst, dst) + sems + (dev,)

    def gather_event(self, i, p, s, g=None):
        h = hops(STREAMS[i][0], p)
        ways = [(kind, way) for kind in (0, 1) for way in (0, 1)]
        if s == h:
            for kind, way in ways:
                self.remote(*self.gather_copy(i, p, g, way, kind, h - kind)[1]).wait_recv()
            return
        for kind, way in ways:
            if s == 0:
                self.send(*self.gather_copy(i, p, g, way, kind, 1)[0])
            elif s < h - kind:
                self.remote(*self.gather_copy(i, p, g, way, kind, s)[1]).wait_recv()
                self.send(*self.gather_copy(i, p, g, way, kind, s + 1)[0])

    def reduce_copy(self, i, p, g, way, kind, hop):
        order = STREAMS[i][0]
        w = SIZE[order[p - 1]] // 2
        half = way if kind == 0 else 1 - way
        tail = pl.ds(half * w, w)
        at = (way, hop - 1, slice(None), tail) if p == 1 else (g, way, hop - 1, tail)
        sem = (i, 0 if p == 1 else 1 + g, way, kind, hop - 1)
        return (
            self.rs_out[i][p].at[at],
            self.rs_in[i][p].at[at],
            self.rs_send.at[sem],
            self.rs_recv.at[sem],
            self.dev(**{order[p]: 1 - 2 * way}),
        )

    def over(self, p, lo, size, body):
        if p == 2:
            for r in range(lo, lo + size):
                body((r,))
        else:
            body((pl.ds(lo, size),))

    def reduce_event(self, i, p, s, g=None):
        order = STREAMS[i][0]
        a = order[p]
        n, w, h = SIZE[a], SIZE[order[p - 1]] // 2, hops(order, p)
        part, out, got = self.part[i], self.rs_out[i][p], self.rs_in[i][p]
        base = (slice(None), self.me[order[2]]) if p == 1 else (g,)
        slot = (lambda way, e: (way, e, slice(None))) if p == 1 else (lambda way, e: (g, way, e))
        ways = [(kind, way) for kind in (0, 1) for way in (0, 1)]
        if s == h:
            for kind, way in ways:
                self.remote(*self.reduce_copy(i, p, g, way, kind, h - kind)).wait_recv()
            mine = base + (self.me[a],)
            for half in (0, 1):
                far, near = slot(half, h - 1), slot(1 - half, h - 2)

                def add(r):
                    part[mine + r] = part[mine + r] + (got[far + r].astype(F32) + got[near + r].astype(F32))

                self.over(p, half * w, w, add)
            return
        for kind, way in ways:
            if s and s >= h - kind:
                continue
            if s:
                self.remote(*self.reduce_copy(i, p, g, way, kind, s)).wait_recv()
            half = way if kind == 0 else 1 - way
            d = h - kind - s
            idx = base + (lax.rem(self.me[a] + (1 - 2 * way) * d + n, n),)

            def put(r):
                v = part[idx + r]
                if s:
                    v = v + got[slot(way, s - 1) + r].astype(F32)
                out[slot(way, s) + r] = v.astype(BF16)

            self.over(p, half * w, w, put)
            self.send(*self.reduce_copy(i, p, g, way, kind, s + 1))

    def collect_copy(self, g, a, d):
        n = SIZE[a]
        to = lax.rem(self.me[a] + d, n)
        sems = self.last_sem[a]
        return self.remote(
            self.last_out[a].at[g, to],
            self.last_in[a].at[self.me[a], self.core],
            sems.at[0, g, d],
            sems.at[1, self.core, d],
            self.dev(core=g, **{a: d}),
        )

    def collect_send(self, g, a):
        col = WIDE[a][0]
        out = self.last_out[a]
        for i in range(NS):
            order, off, width = STREAMS[i]
            if order[0] == a:
                out[g, :, :, off - col : off - col + width] = self.part[i][g, self.me[order[2]], self.me[order[1]]]

        for d in range(SIZE[a]):
            copy = self.collect_copy(g, a, d)
            if d:
                copy.start()
                self.sends.append(copy)
            else:

                @pl.when(self.core != g)
                def _():
                    copy.start()

                @pl.when(self.core == g)
                def _():
                    self.last_in[a][self.me[a], g] = out[g, self.me[a]]

    def collect_wait(self, g, a):
        n = SIZE[a]
        col, width = WIDE[a]
        sems = self.last_sem[a]
        buf = self.last_in[a]

        @pl.when(self.core == g)
        def _():
            for d in range(n):
                for c in (g, 1 - g):
                    if d or c != g:
                        slot = buf.at[lax.rem(self.me[a] - d + n, n), c]
                        self.remote(
                            slot, slot, sems.at[0, g, d], sems.at[1, c, d], self.dev(core=c, **{a: -d})
                        ).wait_recv()
            for c in (0, 1):
                v = buf[0, c]
                for e in range(1, n):
                    v = v + buf[e, c]
                self.gh[:, c * HALF + col : c * HALF + col + width] = v.astype(BF16)

        @pl.when(self.core != g)
        def _():
            self.collect_copy(g, a, 0).wait_send()

    def piece(self, i, g, y, zl):
        order = STREAMS[i][0]
        return jnp.concatenate(
            [self.buf[i][(g,) + self.at(order, x, y, zh * ZL + zl)] for zh in range(ZH) for x in range(4)], axis=0
        )

    def at(self, order, x, y, z):
        c = {"x": x, "y": y, "z": z} | self.roles(x, y)
        return (c[order[2]], c[order[1]], c[order[0]])

    def hidden_block(self, g, j):
        y, zl = j // ZL, lax.rem(j, ZL)
        return jnp.concatenate([self.piece(i, g, y, zl) for i in range(NS)], axis=1)

    def per_group(self, ref, g):
        v = ref[...].reshape(1, 2 * NQ * ROWS)
        return jnp.concatenate([v[:, (2 * q + g) * ROWS : (2 * q + g + 1) * ROWS] for q in range(NQ)], axis=1)

    def logits(self, g):
        acc = self.lg.at[g]
        acc[...] = jnp.zeros_like(acc)

        @pl.loop(0, NB // BLOCKS)
        def _(b):
            js = [b * BLOCKS + e for e in range(BLOCKS)]
            acc[...] += lax.dot_general(
                jnp.concatenate([self.wv[j] for j in js], axis=1),
                jnp.concatenate([self.hidden_block(g, j) for j in js], axis=1),
                (((1,), (1,)), ((), ())),
                preferred_element_type=F32,
            )

        swap = (acc, self.lg_in.at[g], self.lg_sem.at[0, g], self.lg_sem.at[1, g], self.dev(core=1 - self.core))
        self.send(*swap)
        target, scale = self.per_group(self.tgt, g), self.per_group(self.lw, g)
        yield
        self.remote(*swap).wait_recv()
        logits = acc[...] + self.lg_in[g]
        self.lg_sum[g] = logits
        row = lax.broadcasted_iota(jnp.int32, logits.shape, 0)
        row = row + jnp.where(row < self.shard, self.vocab0, self.vocab0 + 15 * self.shard)
        top = jnp.max(logits, axis=0, keepdims=True)
        total = jnp.sum(jnp.exp(logits - top), axis=0, keepdims=True)
        picked = jnp.sum(jnp.where(row == target, logits, 0.0), axis=0, keepdims=True)
        self.stats_send(g, 0, (top, total, picked))
        yield
        self.stats_send(g, 1, self.stats_merge(g, 0))
        yield
        top, total, picked = self.stats_merge(g, 1)
        lse = top + jnp.log(total)
        self.token_loss[g] = lse - picked
        row = lax.broadcasted_iota(jnp.int32, logits.shape, 0)
        row = row + jnp.where(row < self.shard, self.vocab0, self.vocab0 + 15 * self.shard)
        dl = scale * (jnp.exp(self.lg_sum[g] - lse) - (row == target).astype(F32))
        self.dlt[:, g * 128 : (g + 1) * 128] = dl.astype(BF16)
        self.dlr[g] = dl.T.astype(BF16)

        @pl.loop(0, NB, unroll=BLOCKS)
        def _(j):
            y, zl = j // ZL, lax.rem(j, ZL)
            o = jnp.dot(self.dlr[g], self.wv[j], preferred_element_type=F32)
            for i, (order, off, width) in enumerate(STREAMS):
                for zh in range(ZH):
                    for x in range(4):
                        q = (zh * 4 + x) * ROWS
                        at = (g,) + self.at(order, x, y, zh * ZL + zl)
                        self.part[i][at] = o[q : q + ROWS, off : off + width]

    def stats_moves(self, phase):
        if phase == 0:
            return [(dx, dy, 0) for dx in range(4) for dy in range(4) if dx or dy]
        return [(0, 0, dz) for dz in range(1, 8)]

    def stats_send(self, g, phase, mine):
        buf = (self.st0, self.st1)[phase].at[g]
        own = self.me["x"] * 4 + self.me["y"] if phase == 0 else self.me["z"]
        sems = (self.st0_sem, self.st1_sem)[phase]
        buf[own] = jnp.concatenate(mine + (jnp.zeros((5, 128), F32),), axis=0)
        for e, (dx, dy, dz) in enumerate(self.stats_moves(phase)):
            self.send(buf.at[own], buf.at[own], sems.at[0, g, e], sems.at[1, g, e], self.dev(x=dx, y=dy, z=dz))

    def stats_merge(self, g, phase):
        buf = (self.st0, self.st1)[phase].at[g]
        sems = (self.st0_sem, self.st1_sem)[phase]
        moves = self.stats_moves(phase)
        for e, (dx, dy, dz) in enumerate(moves):
            if phase == 0:
                src = lax.rem(self.me["x"] - dx + 4, 4) * 4 + lax.rem(self.me["y"] - dy + 4, 4)
            else:
                src = lax.rem(self.me["z"] - dz + 8, 8)
            self.remote(
                buf.at[src], buf.at[src], sems.at[0, g, e], sems.at[1, g, e], self.dev(x=dx, y=dy, z=dz)
            ).wait_recv()
        tiles = [buf[e] for e in range(len(moves) + 1)]
        top = tiles[0][0:1]
        for t in tiles[1:]:
            top = jnp.maximum(top, t[0:1])
        total = picked = jnp.zeros_like(top)
        for t in tiles:
            total = total + t[1:2] * jnp.exp(t[0:1] - top)
            picked = picked + t[2:3]
        return (top, total, picked)

    def drain(self):
        copies, self.sends = self.sends, []
        return copies

    def pipeline(self):
        both = LONG + SHORT
        ag = lambda streams, s, g: [self.gather_event(i, 2, s, g) for i in streams]
        rs = lambda streams, s, g: [self.reduce_event(i, 2, s, g) for i in streams]
        for i, (order, off, width) in enumerate(STREAMS):
            col = off - WIDE[order[0]][0]
            for g in (0, 1):
                self.buf[i][g, self.me[order[2]], self.me[order[1]]] = self.first[order[0]][g, :, :, col : col + width]
            self.gather_event(i, 1, 0)
        for i in range(NS):
            self.gather_event(i, 1, 1)
        for i in both:
            self.gather_event(i, 1, 2)
            self.gather_event(i, 2, 0, 0)

        @pl.loop(0, NB)
        def _(j):
            self.weight_copies(j)[1].start()

        ag(LONG, 1, 0)
        ag(SHORT, 1, 0)
        ag(LONG, 2, 0)
        ag(SHORT, 0, 1)
        ag(LONG, 3, 0)
        ag(LONG, 0, 1)
        ag(SHORT, 2, 0)
        ag(LONG, 4, 0)
        self.wait_weight()
        zero, one, grads = self.logits(0), self.logits(1), self.grad_quarters()
        next(zero)
        ag(LONG, 1, 1)
        ag(SHORT, 1, 1)
        next(zero)
        ag(LONG, 2, 1)
        next(zero)
        ag(LONG, 3, 1)
        next(zero, None)
        rs(both, 0, 0)
        ag(SHORT, 2, 1)
        ag(LONG, 4, 1)
        next(one)
        rs(LONG, 1, 0)
        rs(SHORT, 1, 0)
        next(one)
        rs(LONG, 2, 0)
        next(one)
        rs(LONG, 3, 0)
        next(one, None)
        early = self.drain()
        rs(both, 0, 1)
        next(grads)
        rs(SHORT, 2, 0)
        rs(LONG, 4, 0)
        rs(LONG, 1, 1)
        next(grads)
        rs(SHORT, 1, 1)
        next(grads)
        rs(LONG, 2, 1)
        next(grads)
        rs(LONG, 3, 1)
        for copy in early:
            copy.wait_send()
        for streams, h in ((SHORT, 2), (LONG, 4)):
            for i in streams:
                self.reduce_event(i, 2, h, 1)
                self.reduce_event(i, 1, 0)
        for i in SHORT + LONG:
            self.reduce_event(i, 1, 1)
        for i in SHORT:
            self.reduce_event(i, 1, 2)
        for g in (0, 1):
            self.collect_send(g, "z")
        for i in LONG:
            self.reduce_event(i, 1, 2)
        for g in (0, 1):
            self.collect_send(g, "y")
        rows = [v[:, q * ROWS : (q + 1) * ROWS] for q in range(NQ) for v in self.token_loss]
        self.loss[...] = jnp.concatenate(rows, axis=1).reshape(2 * NQ * ROWS)
        for copy in self.drain():
            copy.wait_send()
        for a in ("z", "y"):
            for g in (0, 1):
                self.collect_wait(g, a)

    def weight_copies(self, j):
        c, other = self.core, 1 - self.core
        rows = pl.ds(pl.multiple_of(c * self.shard, 16), self.shard)
        cols = lambda h: pl.ds(pl.multiple_of(j * FULL + h * HALF, HALF), HALF)
        theirs = pl.ds(pl.multiple_of(other * self.shard, 16), self.shard)
        local = pltpu.make_async_copy(self.w.at[:, cols(c)], self.wv.at[j, rows], self.w_sem.at[0, j])
        out = self.remote(
            self.w.at[:, cols(other)], self.wv.at[j, rows], self.w_sem.at[1, j], self.w_sem.at[2, j], self.dev(core=other)
        )
        arrive = self.remote(
            self.w.at[:, cols(other)], self.wv.at[j, theirs], self.w_sem.at[1, j], self.w_sem.at[2, j], self.dev(core=other)
        )
        return local, out, arrive

    def wait_weight(self):
        @pl.loop(0, NB)
        def _(j):
            local, out, arrive = self.weight_copies(j)
            local.wait()
            out.wait_send()
            arrive.wait_recv()

    def grad_copies(self, j):
        c, other = self.core, 1 - self.core
        cols = lambda h: pl.ds(pl.multiple_of(j * FULL + h * HALF, HALF), HALF)
        src = lambda h: self.gwb.at[j, pl.ds(pl.multiple_of(h * self.shard, 16), self.shard)]
        local = pltpu.make_async_copy(src(c), self.gw.at[:, cols(c)], self.g_sem.at[0, j])
        dev = self.dev(core=other)
        out = self.remote(src(other), self.gw.at[:, cols(c)], self.g_sem.at[1, j], self.g_sem.at[2, j], dev)
        arrive = self.remote(src(other), self.gw.at[:, cols(other)], self.g_sem.at[1, j], self.g_sem.at[2, j], dev)
        return local, out, arrive

    def grad_weight(self, lo, hi):
        @pl.loop(lo, hi, unroll=BLOCKS)
        def _(j):
            h = jnp.concatenate([self.hidden_block(0, j), self.hidden_block(1, j)], axis=0)
            o = jnp.dot(self.dlt[...], h, preferred_element_type=F32)
            self.gwb[j] = o.astype(BF16)
            local, out, _ = self.grad_copies(j)
            local.start()
            out.start()

    def grad_quarters(self):
        for q in range(4):
            self.grad_weight(q * (NB // 4), (q + 1) * (NB // 4))
            yield

    def run(self):
        other = 1 - self.core
        barrier = pltpu.get_barrier_semaphore()
        peers = [dict(x=dx, y=dy) for dx in range(4) for dy in range(4) if dx or dy]
        peers += [dict(z=dz) for dz in range(1, 8)]
        peers += [dict(core=other, z=dz) for dz in range(8)]
        peers += [dict(core=other, y=dy) for dy in range(1, 4)]
        for d in peers:
            pl.semaphore_signal(barrier, inc=1, device_id=self.dev(**d), device_id_type=MESH)
        for a in ("z", "y"):
            self.spread_copy(a, 0, 0)[0].start()

        @pl.loop(0, NB)
        def _(j):
            self.weight_copies(j)[0].start()

        pl.semaphore_wait(barrier, len(peers))
        self.spread()
        self.spread_wait()
        self.token_loss = [None, None]
        self.pipeline()

        @pl.loop(0, NB)
        def _(j):
            local, out, arrive = self.grad_copies(j)
            local.wait()
            out.wait_send()
            arrive.wait_recv()


def scratch(shard):
    dma = pltpu.SemaphoreType.DMA
    rows = 2 * shard
    out = {
        "wv": pltpu.VMEM((NB, rows, HALF), BF16),
        "lg": pltpu.VMEM((2, rows, 128), F32),
        "lg_in": pltpu.VMEM((2, rows, 128), F32),
        "lg_sum": pltpu.VMEM((2, rows, 128), F32),
        "st0": pltpu.VMEM((2, 16, 8, 128), F32),
        "st1": pltpu.VMEM((2, 8, 8, 128), F32),
        "dlt": pltpu.VMEM((rows, 256), BF16),
        "dlr": pltpu.VMEM((2, 128, rows), BF16),
        "gwb": pltpu.VMEM((NB, rows, HALF), BF16),
        "ag_send": dma((NS, 3, 2, 2, 4)),
        "ag_recv": dma((NS, 3, 2, 2, 4)),
        "rs_send": dma((NS, 3, 2, 2, 4)),
        "rs_recv": dma((NS, 3, 2, 2, 4)),
        "lg_sem": dma((2, 2)),
        "st0_sem": dma((2, 2, 15)),
        "st1_sem": dma((2, 2, 7)),
        "w_sem": dma((3, NB)),
        "g_sem": dma((3, NB)),
    }
    for a in ("z", "y"):
        n, width = SIZE[a], WIDE[a][1]
        out[f"first{a}"] = pltpu.VMEM((2, n, ROWS, width), BF16)
        out[f"first_sem{a}"] = dma((2, 2, n))
        out[f"last_out{a}"] = pltpu.VMEM((2, n, ROWS, width), F32)
        out[f"last_in{a}"] = pltpu.VMEM((n, 2, ROWS, width), F32)
        out[f"last_sem{a}"] = dma((2, 2, n))
    for i, (order, _, width) in enumerate(STREAMS):
        l, m, f = lead(order)
        out[f"buf{i}"] = pltpu.VMEM((2, l, m, f, ROWS, width), BF16)
        out[f"part{i}"] = pltpu.VMEM((2, l, m, f, ROWS, width), F32)
        ring = {p: (2, hops(order, p)) for p in (1, 2)}
        shapes = {1: ring[1] + (2, f, ROWS, width), 2: (2,) + ring[2] + (m, f, ROWS, width)}
        for p in (1, 2):
            out[f"rs_out{i}{p}"] = pltpu.VMEM(shapes[p], BF16)
            out[f"rs_in{i}{p}"] = pltpu.VMEM(shapes[p], BF16)
    return out


def on_device(hidden, head_weight, targets, loss_weight):
    shard, width = head_weight.shape
    spaces = scratch(shard)

    def body(hid, w, tgt, lw, loss, gw, gh, *refs):
        named = dict(zip(spaces, refs))
        args = dict(hid=hid, w=w, tgt=tgt, lw=lw, loss=loss, gw=gw, gh=gh)
        for kind in ("buf", "part"):
            args[kind] = [named.pop(f"{kind}{i}") for i in range(NS)]
        for kind in ("rs_out", "rs_in"):
            args[kind] = [{p: named.pop(f"{kind}{i}{p}") for p in (1, 2)} for i in range(NS)]
        for kind in ("first", "first_sem", "last_out", "last_in", "last_sem"):
            args[kind] = {a: named.pop(f"{kind}{a}") for a in ("z", "y")}
        args.update(named)
        Kernel(shard, args).run()

    vmem, hbm = pl.BlockSpec(memory_space=pltpu.VMEM), pl.BlockSpec(memory_space=pl.ANY)
    loss, gw, gh = pl.pallas_call(
        body,
        out_shape=(
            pltpu.VMEM(loss_weight.shape, F32),
            pltpu.VMEM((shard, width), BF16),
            pltpu.VMEM(hidden.shape, BF16),
        ),
        in_specs=[hbm, hbm, vmem, vmem],
        out_specs=(vmem, vmem, vmem),
        scratch_shapes=list(spaces.values()),
        compiler_params=pltpu.CompilerParams(
            collective_id=0, has_side_effects=True, vmem_limit_bytes=56 * 1024 * 1024
        ),
        cost_estimate=pl.CostEstimate(
            flops=6 * shard * width * 256, bytes_accessed=4 * shard * width, transcendentals=2 * shard * 512
        ),
    )(hidden, head_weight, targets, loss_weight)
    return (loss, gw, gh)


def solution(mesh):
    in_specs = (P("section", "tensor"), P(("section", "tensor"), None), P(), P())
    out_specs = (P(), P(("section", "tensor"), None), P("section", "tensor"))
    return jax.shard_map(
        on_device, mesh=mesh, in_specs=in_specs, out_specs=out_specs, check_vma=False
    )
```

```python
import math

import jax
import jax.numpy as jnp
from jax import lax
from jax.experimental import pallas as pl
from jax.experimental.pallas import tpu as pltpu
from jax.sharding import PartitionSpec as P

MESH = pl.DeviceIdType.MESH
F32, BF16 = jnp.float32, jnp.bfloat16
SIZE = {"x": 4, "y": 4, "z": 8, "a": 4, "b": 4}
ZH, ZL = 2, 4
NB = SIZE["y"] * ZL
NQ = ZH * SIZE["x"]
ROWS = 16
FULL, HALF = 1024, 512
STREAMS = (
    (("z", "b", "a"), 0, 256),
    (("z", "a", "b"), 256, 128),
    (("y", "x", "z"), 384, 128),
)
NS = len(STREAMS)
WIDE = {"z": (0, 384), "y": (384, 128)}
LONG = [i for i in range(NS) if STREAMS[i][0][2] == "z"]
SHORT = [i for i in range(NS) if i not in LONG]
BLOCKS = 2


def flat(ref, idx, count):
    dims = ref.shape[:-1]
    start, rows = 0, math.prod(dims[len(idx) :])
    for e, n in zip(idx, dims):
        start = start * n + e
    start = pl.multiple_of(start * rows, 32)
    return ref.reshape(math.prod(dims), ref.shape[-1]).at[pl.ds(start, count * rows)]


def lead(order):
    f, m, l = (SIZE[a] for a in order)
    return (l, m, f)


def hops(order, p):
    return SIZE[order[p]] // 2


class Kernel:
    def __init__(self, shard, refs):
        self.shard = shard
        self.__dict__.update(refs)
        sec, ten = lax.axis_index("section"), lax.axis_index("tensor")
        self.core = lax.rem(sec, 2)
        z = (sec // 8) * 4 + lax.rem(ten, 4)
        x, y = lax.rem(sec // 2, 4), ten // 4
        self.me = {"x": x, "y": y, "z": z} | self.roles(x, y)
        self.vocab0 = ((sec - self.core) * 16 + ten) * shard

    def roles(self, x, y):
        return {"a": jnp.where(self.core == 0, y, x), "b": jnp.where(self.core == 0, x, y)}

    def dev(self, core=None, **move):
        c = dict(self.me)
        for a, d in move.items():
            c[a] = lax.rem(c[a] + d + SIZE[a], SIZE[a])
            if a in ("a", "b"):
                first = self.core == (0 if a == "b" else 1)
                c["x"], c["y"] = jnp.where(first, c[a], c["x"]), jnp.where(first, c["y"], c[a])
        core = self.core if core is None else core
        return ((c["z"] // 4) * 8 + c["x"] * 2 + core, c["y"] * 4 + lax.rem(c["z"], 4))

    def remote(self, src, dst, ssem, rsem, device):
        return pltpu.make_async_remote_copy(
            src_ref=src, dst_ref=dst, send_sem=ssem, recv_sem=rsem, device_id=device, device_id_type=MESH
        )

    def send(self, *args):
        self.remote(*args).start()

    def settle(self, ref, sem):
        pltpu.make_async_copy(ref, ref, sem).wait()

    def spread_own(self, a):
        col, width = WIDE[a]
        src = self.hid.at[:, pl.ds(pl.multiple_of(self.core * HALF + col, 128), width)]
        return pltpu.make_async_copy(src, self.first[a].at[self.core, self.me[a]], self.first_sem[a].at[1])

    def spread(self):
        for a in ("z", "y"):
            n = SIZE[a]
            col, width = WIDE[a]

            @pl.loop(1, 2 * n)
            def _(e):
                to_core = lax.rem(self.core + e, 2)
                src = self.hid.at[:, pl.ds(pl.multiple_of(to_core * HALF + col, 128), width)]
                dst = self.first[a].at[self.core, self.me[a]]
                dev = self.dev(core=to_core, **{a: e // 2})
                self.send(src, dst, self.first_sem[a].at[0], self.first_sem[a].at[1], dev)

    def first_flat(self, a):
        return self.first[a].reshape(2 * SIZE[a], ROWS, WIDE[a][1])

    def spread_wait(self):
        for a in ("z", "y"):
            self.settle(self.first[a], self.first_sem[a].at[1])

    def settle_all(self, ref, sem, count):
        self.settle(ref.at[pl.ds(0, count)], sem)

    def gather_copy(self, i, p, way, kind, hop):
        order = STREAMS[i][0]
        a = order[p]
        n, w = SIZE[a], SIZE[order[p - 1]] // 2
        sign = 1 - 2 * way
        half = way if kind == 0 else 1 - way
        idx = (self.me[order[2]],) if p == 1 else ()
        out = lax.rem(self.me[a] - sign * (hop - 1) + n, n)
        got = lax.rem(self.me[a] - sign * hop + n, n)
        at = half * w
        sems = (self.ag_send.at[i, p - 1], self.ag_recv.at[i, p - 1, way, kind, hop - 1])
        dev = self.dev(**{a: sign})
        src, dst = (flat(self.buf[i], idx + (e, at), w) for e in (out, got))
        return (src, src) + sems + (dev,), (dst, dst) + sems + (dev,)

    def gather_event(self, i, p, s):
        h = hops(STREAMS[i][0], p)
        ways = [(kind, way) for kind in (0, 1) for way in (0, 1)]
        if s == h:
            for kind, way in ways:
                self.remote(*self.gather_copy(i, p, way, kind, h - kind)[1]).wait_recv()
            return
        for kind, way in ways:
            if s == 0:
                self.send(*self.gather_copy(i, p, way, kind, 1)[0])
            elif s < h - kind:
                self.remote(*self.gather_copy(i, p, way, kind, s)[1]).wait_recv()
                self.send(*self.gather_copy(i, p, way, kind, s + 1)[0])

    def reduce_copy(self, i, p, way, kind, hop):
        order = STREAMS[i][0]
        w = SIZE[order[p - 1]] // 2
        half = way if kind == 0 else 1 - way
        at = (way, hop - 1, half * w)
        return (
            flat(self.rs_out[i][p], at, w),
            flat(self.rs_in[i][p], at, w),
            self.rs_send.at[i, p - 1],
            self.rs_recv.at[i, p - 1, way, kind, hop - 1],
            self.dev(**{order[p]: 1 - 2 * way}),
        )

    def over(self, p, lo, size, body):
        if p == 2:
            for r in range(lo, lo + size):
                body((r,))
        else:
            body((pl.ds(lo, size),))

    def reduce_event(self, i, p, s):
        order = STREAMS[i][0]
        a = order[p]
        n, w, h = SIZE[a], SIZE[order[p - 1]] // 2, hops(order, p)
        part, out, got = self.part[i], self.rs_out[i][p], self.rs_in[i][p]
        base = (self.me[order[2]],) if p == 1 else ()
        ways = [(kind, way) for kind in (0, 1) for way in (0, 1)]
        if s == h:
            for kind, way in ways:
                self.remote(*self.reduce_copy(i, p, way, kind, h - kind)).wait_recv()
            mine = base + (self.me[a],)
            for half in (0, 1):
                far, near = (half, h - 1), (1 - half, h - 2)

                def add(r):
                    part[mine + r] = part[mine + r] + (got[far + r].astype(F32) + got[near + r].astype(F32))

                self.over(p, half * w, w, add)
            return
        for kind, way in ways:
            if s and s >= h - kind:
                continue
            if s:
                self.remote(*self.reduce_copy(i, p, way, kind, s)).wait_recv()
            half = way if kind == 0 else 1 - way
            d = h - kind - s
            idx = base + (lax.rem(self.me[a] + (1 - 2 * way) * d + n, n),)

            def put(r):
                v = part[idx + r]
                if s:
                    v = v + got[(way, s - 1) + r].astype(F32)
                out[(way, s) + r] = v.astype(BF16)

            self.over(p, half * w, w, put)
            self.send(*self.reduce_copy(i, p, way, kind, s + 1))

    def collect_copy(self, g, a, d):
        to = lax.rem(self.me[a] + d, SIZE[a])
        sem = self.last_sem[a]
        slot = self.last_in[a].at[self.me[a] * 2 + self.core]
        return self.remote(self.last_out[a].at[g, to], slot, sem.at[0, g], sem.at[1, 0], self.dev(core=g, **{a: d}))

    def collect_send(self, g, a):
        col = WIDE[a][0]
        out = self.last_out[a]
        for i in range(NS):
            order, off, width = STREAMS[i]
            if order[0] == a:
                mine = self.part[i].at[self.me[order[2]], self.me[order[1]]]
                out[g, :, :, off - col : off - col + width] = mine[:, g * ROWS : (g + 1) * ROWS]

        @pl.loop(1, SIZE[a])
        def _(d):
            self.collect_copy(g, a, d).start()

        @pl.when(self.core != g)
        def _():
            self.collect_copy(g, a, 0).start()

        @pl.when(self.core == g)
        def _():
            self.last_in[a][self.me[a] * 2 + g] = out[g, self.me[a]]

    def collect_wait(self, g, a):
        n = SIZE[a]
        col, width = WIDE[a]
        sem = self.last_sem[a]
        buf = self.last_in[a]

        @pl.when(self.core == g)
        def _():
            self.settle_all(self.last_out[a].at[g], sem.at[0, g], n - 1)
            self.settle_all(buf, sem.at[1, 0], 2 * n - 1)
            for c in (0, 1):
                v = buf[c]
                for e in range(1, n):
                    v = v + buf[2 * e + c]
                self.gh[:, c * HALF + col : c * HALF + col + width] = v.astype(BF16)

        @pl.when(self.core != g)
        def _():
            self.settle(self.last_out[a].at[g], sem.at[0, g])

    def piece(self, i, y, zl):
        order, _, _ = STREAMS[i]
        return jnp.concatenate([self.buf[i][self.at(order, x, y, zh * ZL + zl)] for zh in range(ZH) for x in range(4)], axis=0)

    def at(self, order, x, y, z):
        c = {"x": x, "y": y, "z": z} | self.roles(x, y)
        return (c[order[2]], c[order[1]], c[order[0]])

    def hidden_block(self, j):
        y, zl = j // ZL, lax.rem(j, ZL)
        return jnp.concatenate([self.piece(i, y, zl) for i in range(NS)], axis=1)

    def gather(self):
        for i, (order, off, width) in enumerate(STREAMS):
            col = off - WIDE[order[0]][0]
            mine = self.buf[i].at[self.me[order[2]], self.me[order[1]]]
            for g in (0, 1):
                mine[:, g * ROWS : (g + 1) * ROWS] = self.first[order[0]][g, :, :, col : col + width]
            self.gather_event(i, 1, 0)
        for i in range(NS):
            self.gather_event(i, 1, 1)
        for i in LONG + SHORT:
            self.gather_event(i, 1, 2)
            self.gather_event(i, 2, 0)

        @pl.loop(0, NB)
        def _(j):
            self.weight_copies(j)[1]().start()

        for streams, s in ((LONG, 1), (SHORT, 1), (LONG, 2), (LONG, 3), (SHORT, 2), (LONG, 4)):
            for i in streams:
                self.gather_event(i, 2, s)

    def settle_ring(self, sems, phases):
        for i, (order, _, _) in enumerate(STREAMS):
            for p in phases:
                ref = self.buf[i].at[0] if p == 1 else self.buf[i]
                self.settle_all(ref, sems.at[i, p - 1], SIZE[order[p]] - 1)

    def reduce(self):
        for i in LONG + SHORT:
            self.reduce_event(i, 2, 0)
        self.grad_weight(0, NB // 2)
        for i in LONG:
            self.reduce_event(i, 2, 1)
        for i in SHORT:
            self.reduce_event(i, 2, 1)
        for i in LONG:
            self.reduce_event(i, 2, 2)
        self.grad_weight(NB // 2, NB)
        for i in LONG:
            self.reduce_event(i, 2, 3)
        for a in ("z", "y"):
            self.settle_all(self.first_flat(a), self.first_sem[a].at[0], 2 * SIZE[a] - 1)
        self.settle_all(self.st0, self.st0_sem.at[0], 15)
        self.settle_all(self.st1, self.st1_sem.at[0], 7)
        self.settle(self.lg, self.lg_sem.at[0])
        self.settle_ring(self.ag_send, (1, 2))
        for i in SHORT:
            self.reduce_event(i, 2, 2)
            self.reduce_event(i, 1, 0)
        for i in LONG:
            self.reduce_event(i, 2, 4)
            self.reduce_event(i, 1, 0)
        for i in SHORT + LONG:
            self.reduce_event(i, 1, 1)
        for i in SHORT:
            self.reduce_event(i, 1, 2)
        for g in (0, 1):
            self.collect_send(g, "z")
        for i in LONG:
            self.reduce_event(i, 1, 2)
        for g in (0, 1):
            self.collect_send(g, "y")
        self.settle_ring(self.rs_send, (2, 1))
        half = self.gwb.at[:, pl.ds(0, self.shard)]
        for e in range(3):
            self.settle(half, self.g_sem.at[e])
        for a in ("z", "y"):
            for g in (0, 1):
                self.collect_wait(g, a)

    def loss_and_grads(self):
        self.wait_weight()
        acc = self.lg
        acc[...] = jnp.zeros_like(acc)

        @pl.loop(0, NB // BLOCKS)
        def _(b):
            js = [b * BLOCKS + e for e in range(BLOCKS)]
            acc[...] += lax.dot_general(
                jnp.concatenate([self.wv[j] for j in js], axis=1),
                jnp.concatenate([self.hidden_block(j) for j in js], axis=1),
                (((1,), (1,)), ((), ())),
                preferred_element_type=F32,
            )

        swap = (acc, self.lg_in, self.lg_sem.at[0], self.lg_sem.at[1], self.dev(core=1 - self.core))
        self.send(*swap)
        target, scale = self.tgt[...].reshape(1, -1), self.lw[...].reshape(1, -1)
        self.remote(*swap).wait_recv()
        logits = acc[...] + self.lg_in[...]
        self.lg_sum[...] = logits
        row = lax.broadcasted_iota(jnp.int32, logits.shape, 0)
        row = row + jnp.where(row < self.shard, self.vocab0, self.vocab0 + 15 * self.shard)
        hit = row == target
        top = jnp.max(logits, axis=0, keepdims=True)
        total = jnp.sum(jnp.exp(logits - top), axis=0, keepdims=True)
        picked = jnp.sum(jnp.where(hit, logits, 0.0), axis=0, keepdims=True)
        top, total, picked = self.stats(1, self.stats(0, (top, total, picked)))
        lse = top + jnp.log(total)
        self.loss[...] = (lse - picked).reshape(2 * NQ * ROWS)
        dl = scale * (jnp.exp(self.lg_sum[...] - lse) - (row == target).astype(F32))
        self.dlt[...] = dl.astype(BF16)
        self.dlr[...] = dl.T.astype(BF16)

        @pl.loop(0, NB, unroll=BLOCKS)
        def _(j):
            y, zl = j // ZL, lax.rem(j, ZL)
            o = jnp.dot(self.dlr[...], self.wv[j], preferred_element_type=F32)
            for i, (order, off, width) in enumerate(STREAMS):
                for zh in range(ZH):
                    for x in range(4):
                        q = (zh * 4 + x) * 2 * ROWS
                        self.part[i][self.at(order, x, y, zh * ZL + zl)] = o[q : q + 2 * ROWS, off : off + width]

    def stats(self, phase, mine):
        buf = (self.st0, self.st1)[phase]
        sem = (self.st0_sem, self.st1_sem)[phase]
        own = self.me["x"] * 4 + self.me["y"] if phase == 0 else self.me["z"]
        n = buf.shape[0]
        buf[own] = jnp.concatenate(mine + (jnp.zeros((5, 256), F32),), axis=0)

        @pl.loop(1, n)
        def _(e):
            dev = self.dev(x=e // 4, y=lax.rem(e, 4)) if phase == 0 else self.dev(z=e)
            self.send(buf.at[own], buf.at[own], sem.at[0], sem.at[1], dev)

        self.settle_all(buf, sem.at[1], n - 1)
        tiles = [buf[e] for e in range(n)]
        top = tiles[0][0:1]
        for t in tiles[1:]:
            top = jnp.maximum(top, t[0:1])
        total = picked = jnp.zeros_like(top)
        for t in tiles:
            total = total + t[1:2] * jnp.exp(t[0:1] - top)
            picked = picked + t[2:3]
        return (top, total, picked)

    def weight_copies(self, j):
        c, other = self.core, 1 - self.core
        rows = pl.ds(pl.multiple_of(c * self.shard, 16), self.shard)
        cols = lambda h: pl.ds(pl.multiple_of(j * FULL + h * HALF, HALF), HALF)
        dst = self.wv.at[j, rows]
        local = pltpu.make_async_copy(self.w.at[:, cols(c)], dst, self.w_sem.at[0])
        out = lambda: self.remote(
            self.w.at[:, cols(other)], dst, self.w_sem.at[1], self.w_sem.at[2], self.dev(core=other)
        )
        return local, out

    def wait_weight(self):
        half = self.wv.at[:, pl.ds(0, self.shard)]
        for e in range(3):
            self.settle(half, self.w_sem.at[e])

    def grad_weight(self, lo, hi):
        c, other = self.core, 1 - self.core

        @pl.loop(lo, hi, unroll=BLOCKS)
        def _(j):
            self.gwb[j] = jnp.dot(self.dlt[...], self.hidden_block(j), preferred_element_type=F32).astype(BF16)
            src = lambda h: self.gwb.at[j, pl.ds(pl.multiple_of(h * self.shard, 16), self.shard)]
            dst = self.gw.at[:, pl.ds(pl.multiple_of(j * FULL + c * HALF, HALF), HALF)]
            pltpu.make_async_copy(src(c), dst, self.g_sem.at[0]).start()
            self.send(src(other), dst, self.g_sem.at[1], self.g_sem.at[2], self.dev(core=other))

    def run(self):
        other = 1 - self.core
        barrier = pltpu.get_barrier_semaphore()
        peers = [dict(x=dx, y=dy) for dx in range(4) for dy in range(4) if dx or dy]
        peers += [dict(z=dz) for dz in range(1, 8)]
        peers += [dict(core=other, z=dz) for dz in range(8)]
        peers += [dict(core=other, y=dy) for dy in range(1, 4)]
        for d in peers:
            pl.semaphore_signal(barrier, inc=1, device_id=self.dev(**d), device_id_type=MESH)
        for a in ("z", "y"):
            self.spread_own(a).start()

        @pl.loop(0, NB)
        def _(j):
            self.weight_copies(j)[0].start()

        pl.semaphore_wait(barrier, len(peers))
        self.spread()
        self.spread_wait()
        self.gather()
        self.loss_and_grads()
        self.reduce()


def scratch(shard):
    dma = pltpu.SemaphoreType.DMA
    rows = 2 * shard
    out = {
        "wv": pltpu.VMEM((NB, rows, HALF), BF16),
        "lg": pltpu.VMEM((rows, 256), F32),
        "lg_in": pltpu.VMEM((rows, 256), F32),
        "lg_sum": pltpu.VMEM((rows, 256), F32),
        "st0": pltpu.VMEM((16, 8, 256), F32),
        "st1": pltpu.VMEM((8, 8, 256), F32),
        "dlt": pltpu.VMEM((rows, 256), BF16),
        "dlr": pltpu.VMEM((256, rows), BF16),
        "gwb": pltpu.VMEM((NB, rows, HALF), BF16),
        "ag_send": dma((NS, 2)),
        "ag_recv": dma((NS, 2, 2, 2, 4)),
        "rs_send": dma((NS, 2)),
        "rs_recv": dma((NS, 2, 2, 2, 4)),
        "lg_sem": dma((2,)),
        "st0_sem": dma((2,)),
        "st1_sem": dma((2,)),
        "w_sem": dma((3,)),
        "g_sem": dma((3,)),
    }
    for a in ("z", "y"):
        n, width = SIZE[a], WIDE[a][1]
        out[f"first{a}"] = pltpu.VMEM((2, n, ROWS, width), BF16)
        out[f"first_sem{a}"] = dma((2,))
        out[f"last_out{a}"] = pltpu.VMEM((2, n, ROWS, width), F32)
        out[f"last_in{a}"] = pltpu.VMEM((2 * n, ROWS, width), F32)
        out[f"last_sem{a}"] = dma((2, 2))
    for i, (order, _, width) in enumerate(STREAMS):
        l, m, f = lead(order)
        out[f"buf{i}"] = pltpu.VMEM((l, m, f, 2 * ROWS, width), BF16)
        out[f"part{i}"] = pltpu.VMEM((l, m, f, 2 * ROWS, width), F32)
        chunk = {2: (m, f, 2 * ROWS, width), 1: (f, 2 * ROWS, width)}
        for p in (1, 2):
            shape = (2, hops(order, p)) + chunk[p]
            out[f"rs_out{i}{p}"] = pltpu.VMEM(shape, BF16)
            out[f"rs_in{i}{p}"] = pltpu.VMEM(shape, BF16)
    return out


def on_device(hidden, head_weight, targets, loss_weight):
    shard, width = head_weight.shape
    spaces = scratch(shard)

    def body(hid, w, tgt, lw, loss, gw, gh, *refs):
        named = dict(zip(spaces, refs))
        args = dict(hid=hid, w=w, tgt=tgt, lw=lw, loss=loss, gw=gw, gh=gh)
        for kind in ("buf", "part"):
            args[kind] = [named.pop(f"{kind}{i}") for i in range(NS)]
        for kind in ("rs_out", "rs_in"):
            args[kind] = [{p: named.pop(f"{kind}{i}{p}") for p in (1, 2)} for i in range(NS)]
        for kind in ("first", "first_sem", "last_out", "last_in", "last_sem"):
            args[kind] = {a: named.pop(f"{kind}{a}") for a in ("z", "y")}
        args.update(named)
        Kernel(shard, args).run()

    vmem, hbm = pl.BlockSpec(memory_space=pltpu.VMEM), pl.BlockSpec(memory_space=pl.ANY)
    loss, gw, gh = pl.pallas_call(
        body,
        out_shape=(
            pltpu.VMEM(loss_weight.shape, F32),
            pltpu.VMEM((shard, width), BF16),
            pltpu.VMEM(hidden.shape, BF16),
        ),
        in_specs=[hbm, hbm, vmem, vmem],
        out_specs=(vmem, vmem, vmem),
        scratch_shapes=list(spaces.values()),
        compiler_params=pltpu.CompilerParams(
            collective_id=0, has_side_effects=True, vmem_limit_bytes=56 * 1024 * 1024
        ),
        cost_estimate=pl.CostEstimate(
            flops=6 * shard * width * 256, bytes_accessed=4 * shard * width, transcendentals=2 * shard * 512
        ),
    )(hidden, head_weight, targets, loss_weight)
    return (loss, gw, gh)


def solution(mesh):
    in_specs = (P("section", "tensor"), P(("section", "tensor"), None), P(), P())
    out_specs = (P(), P(("section", "tensor"), None), P("section", "tensor"))
    return jax.shard_map(
        on_device, mesh=mesh, in_specs=in_specs, out_specs=out_specs, check_vma=False
    )
```

```python
import math

import jax
import jax.numpy as jnp
from jax import lax
from jax.experimental import pallas as pl
from jax.experimental.pallas import tpu as pltpu
from jax.sharding import PartitionSpec as P

MESH = pl.DeviceIdType.MESH
F32, BF16 = jnp.float32, jnp.bfloat16
SIZE = {"x": 4, "y": 4, "z": 8, "a": 4, "b": 4}
ZH, ZL = 2, 4
NB = SIZE["y"] * ZL
NQ = ZH * SIZE["x"]
ROWS = 16
FULL, HALF = 1024, 512
STREAMS = (
    (("z", "b", "a"), 0, 256),
    (("z", "a", "b"), 256, 256),
)
NS = len(STREAMS)
WIDE = {"z": (0, 512)}
BLOCKS = 2


def flat(ref, idx, count):
    dims = ref.shape[:-1]
    start, rows = 0, math.prod(dims[len(idx) :])
    for e, n in zip(idx, dims):
        start = start * n + e
    start = pl.multiple_of(start * rows, 32)
    return ref.reshape(math.prod(dims), ref.shape[-1]).at[pl.ds(start, count * rows)]


def lead(order):
    f, m, l = (SIZE[a] for a in order)
    return (l, m, f)


def hops(order, p):
    return SIZE[order[p]] // 2


class Kernel:
    def __init__(self, shard, refs):
        self.shard = shard
        self.__dict__.update(refs)
        sec, ten = lax.axis_index("section"), lax.axis_index("tensor")
        self.core = lax.rem(sec, 2)
        z = (sec // 8) * 4 + lax.rem(ten, 4)
        x, y = lax.rem(sec // 2, 4), ten // 4
        self.me = {"x": x, "y": y, "z": z} | self.roles(x, y)
        self.vocab0 = ((sec - self.core) * 16 + ten) * shard

    def roles(self, x, y):
        return {"a": jnp.where(self.core == 0, y, x), "b": jnp.where(self.core == 0, x, y)}

    def dev(self, core=None, **move):
        c = dict(self.me)
        for a, d in move.items():
            c[a] = lax.rem(c[a] + d + SIZE[a], SIZE[a])
            if a in ("a", "b"):
                first = self.core == (0 if a == "b" else 1)
                c["x"], c["y"] = jnp.where(first, c[a], c["x"]), jnp.where(first, c["y"], c[a])
        core = self.core if core is None else core
        return ((c["z"] // 4) * 8 + c["x"] * 2 + core, c["y"] * 4 + lax.rem(c["z"], 4))

    def remote(self, src, dst, ssem, rsem, device):
        return pltpu.make_async_remote_copy(
            src_ref=src, dst_ref=dst, send_sem=ssem, recv_sem=rsem, device_id=device, device_id_type=MESH
        )

    def send(self, *args):
        self.remote(*args).start()

    def settle(self, ref, sem):
        pltpu.make_async_copy(ref, ref, sem).wait()

    def spread_own(self, a):
        col, width = WIDE[a]
        src = self.hid.at[:, pl.ds(pl.multiple_of(self.core * HALF + col, 128), width)]
        return pltpu.make_async_copy(src, self.first[a].at[self.core, self.me[a]], self.first_sem[a].at[1])

    def spread(self):
        for a in WIDE:
            n = SIZE[a]
            col, width = WIDE[a]

            @pl.loop(1, 2 * n)
            def _(e):
                to_core = lax.rem(self.core + e, 2)
                src = self.hid.at[:, pl.ds(pl.multiple_of(to_core * HALF + col, 128), width)]
                dst = self.first[a].at[self.core, self.me[a]]
                dev = self.dev(core=to_core, **{a: e // 2})
                self.send(src, dst, self.first_sem[a].at[0], self.first_sem[a].at[1], dev)

    def first_flat(self, a):
        return self.first[a].reshape(2 * SIZE[a], ROWS, WIDE[a][1])

    def spread_wait(self):
        for a in WIDE:
            self.settle(self.first[a], self.first_sem[a].at[1])

    def settle_all(self, ref, sem, count):
        self.settle(ref.at[pl.ds(0, count)], sem)

    def gather_copy(self, i, p, way, kind, hop):
        order = STREAMS[i][0]
        a = order[p]
        n, w = SIZE[a], SIZE[order[p - 1]] // 2
        sign = 1 - 2 * way
        half = way if kind == 0 else 1 - way
        idx = (self.me[order[2]],) if p == 1 else ()
        out = lax.rem(self.me[a] - sign * (hop - 1) + n, n)
        got = lax.rem(self.me[a] - sign * hop + n, n)
        at = half * w
        sems = (self.ag_send.at[i, p - 1], self.ag_recv.at[i, p - 1, way, kind, hop - 1])
        dev = self.dev(**{a: sign})
        src, dst = (flat(self.buf[i], idx + (e, at), w) for e in (out, got))
        return (src, src) + sems + (dev,), (dst, dst) + sems + (dev,)

    def gather_event(self, i, p, s):
        h = hops(STREAMS[i][0], p)
        ways = [(kind, way) for kind in (0, 1) for way in (0, 1)]
        if s == h:
            for kind, way in ways:
                self.remote(*self.gather_copy(i, p, way, kind, h - kind)[1]).wait_recv()
            return
        for kind, way in ways:
            if s == 0:
                self.send(*self.gather_copy(i, p, way, kind, 1)[0])
            elif s < h - kind:
                self.remote(*self.gather_copy(i, p, way, kind, s)[1]).wait_recv()
                self.send(*self.gather_copy(i, p, way, kind, s + 1)[0])

    def reduce_copy(self, i, p, way, kind, hop):
        order = STREAMS[i][0]
        w = SIZE[order[p - 1]] // 2
        half = way if kind == 0 else 1 - way
        at = (way, hop - 1, half * w)
        return (
            flat(self.rs_out[i][p], at, w),
            flat(self.rs_in[i][p], at, w),
            self.rs_send.at[i, p - 1],
            self.rs_recv.at[i, p - 1, way, kind, hop - 1],
            self.dev(**{order[p]: 1 - 2 * way}),
        )

    def over(self, p, lo, size, body):
        if p == 2:
            for r in range(lo, lo + size):
                body((r,))
        else:
            body((pl.ds(lo, size),))

    def reduce_event(self, i, p, s):
        order = STREAMS[i][0]
        a = order[p]
        n, w, h = SIZE[a], SIZE[order[p - 1]] // 2, hops(order, p)
        part, out, got = self.part[i], self.rs_out[i][p], self.rs_in[i][p]
        base = (self.me[order[2]],) if p == 1 else ()
        ways = [(kind, way) for kind in (0, 1) for way in (0, 1)]
        if s == h:
            for kind, way in ways:
                self.remote(*self.reduce_copy(i, p, way, kind, h - kind)).wait_recv()
            mine = base + (self.me[a],)
            for half in (0, 1):
                far, near = (half, h - 1), (1 - half, h - 2)

                def add(r):
                    part[mine + r] = part[mine + r] + (got[far + r].astype(F32) + got[near + r].astype(F32))

                self.over(p, half * w, w, add)
            return
        for kind, way in ways:
            if s and s >= h - kind:
                continue
            if s:
                self.remote(*self.reduce_copy(i, p, way, kind, s)).wait_recv()
            half = way if kind == 0 else 1 - way
            d = h - kind - s
            idx = base + (lax.rem(self.me[a] + (1 - 2 * way) * d + n, n),)

            def put(r):
                v = part[idx + r]
                if s:
                    v = v + got[(way, s - 1) + r].astype(F32)
                out[(way, s) + r] = v.astype(BF16)

            self.over(p, half * w, w, put)
            self.send(*self.reduce_copy(i, p, way, kind, s + 1))

    def collect_copy(self, g, a, d):
        to = lax.rem(self.me[a] + d, SIZE[a])
        sem = self.last_sem[a]
        slot = self.last_in[a].at[self.me[a] * 2 + self.core]
        return self.remote(self.last_out[a].at[g, to], slot, sem.at[0, g], sem.at[1, 0], self.dev(core=g, **{a: d}))

    def collect_send(self, g, a):
        col = WIDE[a][0]
        out = self.last_out[a]
        for i in range(NS):
            order, off, width = STREAMS[i]
            if order[0] == a:
                mine = self.part[i].at[self.me[order[2]], self.me[order[1]]]
                out[g, :, :, off - col : off - col + width] = mine[:, g * ROWS : (g + 1) * ROWS]

        @pl.loop(1, SIZE[a])
        def _(d):
            self.collect_copy(g, a, d).start()

        @pl.when(self.core != g)
        def _():
            self.collect_copy(g, a, 0).start()

        @pl.when(self.core == g)
        def _():
            self.last_in[a][self.me[a] * 2 + g] = out[g, self.me[a]]

    def collect_wait(self, g, a):
        n = SIZE[a]
        col, width = WIDE[a]
        sem = self.last_sem[a]
        buf = self.last_in[a]

        @pl.when(self.core == g)
        def _():
            self.settle_all(self.last_out[a].at[g], sem.at[0, g], n - 1)
            self.settle_all(buf, sem.at[1, 0], 2 * n - 1)
            for c in (0, 1):
                v = buf[c]
                for e in range(1, n):
                    v = v + buf[2 * e + c]
                self.gh[:, c * HALF + col : c * HALF + col + width] = v.astype(BF16)

        @pl.when(self.core != g)
        def _():
            self.settle(self.last_out[a].at[g], sem.at[0, g])

    def piece(self, i, y, zl):
        order, _, _ = STREAMS[i]
        return jnp.concatenate([self.buf[i][self.at(order, x, y, zh * ZL + zl)] for zh in range(ZH) for x in range(4)], axis=0)

    def at(self, order, x, y, z):
        c = {"x": x, "y": y, "z": z} | self.roles(x, y)
        return (c[order[2]], c[order[1]], c[order[0]])

    def hidden_block(self, j):
        y, zl = j // ZL, lax.rem(j, ZL)
        return jnp.concatenate([self.piece(i, y, zl) for i in range(NS)], axis=1)

    def gather(self):
        for i, (order, off, width) in enumerate(STREAMS):
            col = off - WIDE[order[0]][0]
            mine = self.buf[i].at[self.me[order[2]], self.me[order[1]]]
            for g in (0, 1):
                mine[:, g * ROWS : (g + 1) * ROWS] = self.first[order[0]][g, :, :, col : col + width]
            self.gather_event(i, 1, 0)
        for i in range(NS):
            self.gather_event(i, 1, 1)
        for i in range(NS):
            self.gather_event(i, 1, 2)
            self.gather_event(i, 2, 0)

        @pl.loop(0, NB)
        def _(j):
            self.weight_copies(j)[1]().start()

        for s in (1, 2):
            for i in range(NS):
                self.gather_event(i, 2, s)

    def settle_ring(self, sems, phases):
        for i, (order, _, _) in enumerate(STREAMS):
            for p in phases:
                ref = self.buf[i].at[0] if p == 1 else self.buf[i]
                self.settle_all(ref, sems.at[i, p - 1], SIZE[order[p]] - 1)

    def reduce(self):
        for i in range(NS):
            self.reduce_event(i, 2, 0)
        self.grad_weight(0, NB // 2)
        for i in range(NS):
            self.reduce_event(i, 2, 1)
        self.grad_weight(NB // 2, NB)
        self.settle_all(self.first_flat("z"), self.first_sem["z"].at[0], 2 * SIZE["z"] - 1)
        self.settle_all(self.st0, self.st0_sem.at[0], 15)
        self.settle_all(self.st1, self.st1_sem.at[0], 7)
        self.settle(self.lg, self.lg_sem.at[0])
        self.settle_ring(self.ag_send, (1, 2))
        for i in range(NS):
            self.reduce_event(i, 2, 2)
            self.reduce_event(i, 1, 0)
        for s in (1, 2):
            for i in range(NS):
                self.reduce_event(i, 1, s)
        for g in (0, 1):
            self.collect_send(g, "z")
        self.settle_ring(self.rs_send, (2, 1))
        half = self.gwb.at[:, pl.ds(0, self.shard)]
        for e in range(3):
            self.settle(half, self.g_sem.at[e])
        for g in (0, 1):
            self.collect_wait(g, "z")

    def loss_and_grads(self):
        self.wait_weight()
        acc = self.lg
        acc[...] = jnp.zeros_like(acc)

        @pl.loop(0, NB // BLOCKS)
        def _(b):
            js = [b * BLOCKS + e for e in range(BLOCKS)]
            acc[...] += lax.dot_general(
                jnp.concatenate([self.wv[j] for j in js], axis=1),
                jnp.concatenate([self.hidden_block(j) for j in js], axis=1),
                (((1,), (1,)), ((), ())),
                preferred_element_type=F32,
            )

        swap = (acc, self.lg_in, self.lg_sem.at[0], self.lg_sem.at[1], self.dev(core=1 - self.core))
        self.send(*swap)
        target, scale = self.tgt[...].reshape(1, -1), self.lw[...].reshape(1, -1)
        self.remote(*swap).wait_recv()
        logits = acc[...] + self.lg_in[...]
        self.lg_sum[...] = logits
        row = lax.broadcasted_iota(jnp.int32, logits.shape, 0)
        row = row + jnp.where(row < self.shard, self.vocab0, self.vocab0 + 15 * self.shard)
        hit = row == target
        top = jnp.max(logits, axis=0, keepdims=True)
        total = jnp.sum(jnp.exp(logits - top), axis=0, keepdims=True)
        picked = jnp.sum(jnp.where(hit, logits, 0.0), axis=0, keepdims=True)
        top, total, picked = self.stats(1, self.stats(0, (top, total, picked)))
        lse = top + jnp.log(total)
        self.loss[...] = (lse - picked).reshape(2 * NQ * ROWS)
        dl = scale * (jnp.exp(self.lg_sum[...] - lse) - (row == target).astype(F32))
        self.dlt[...] = dl.astype(BF16)
        self.dlr[...] = dl.T.astype(BF16)

        @pl.loop(0, NB, unroll=BLOCKS)
        def _(j):
            y, zl = j // ZL, lax.rem(j, ZL)
            o = jnp.dot(self.dlr[...], self.wv[j], preferred_element_type=F32)
            for i, (order, off, width) in enumerate(STREAMS):
                for zh in range(ZH):
                    for x in range(4):
                        q = (zh * 4 + x) * 2 * ROWS
                        self.part[i][self.at(order, x, y, zh * ZL + zl)] = o[q : q + 2 * ROWS, off : off + width]

    def stats(self, phase, mine):
        buf = (self.st0, self.st1)[phase]
        sem = (self.st0_sem, self.st1_sem)[phase]
        own = self.me["x"] * 4 + self.me["y"] if phase == 0 else self.me["z"]
        n = buf.shape[0]
        buf[own] = jnp.concatenate(mine + (jnp.zeros((5, 256), F32),), axis=0)

        @pl.loop(1, n)
        def _(e):
            dev = self.dev(x=e // 4, y=lax.rem(e, 4)) if phase == 0 else self.dev(z=e)
            self.send(buf.at[own], buf.at[own], sem.at[0], sem.at[1], dev)

        self.settle_all(buf, sem.at[1], n - 1)
        tiles = [buf[e] for e in range(n)]
        top = tiles[0][0:1]
        for t in tiles[1:]:
            top = jnp.maximum(top, t[0:1])
        total = picked = jnp.zeros_like(top)
        for t in tiles:
            total = total + t[1:2] * jnp.exp(t[0:1] - top)
            picked = picked + t[2:3]
        return (top, total, picked)

    def weight_copies(self, j):
        c, other = self.core, 1 - self.core
        rows = pl.ds(pl.multiple_of(c * self.shard, 16), self.shard)
        cols = lambda h: pl.ds(pl.multiple_of(j * FULL + h * HALF, HALF), HALF)
        dst = self.wv.at[j, rows]
        local = pltpu.make_async_copy(self.w.at[:, cols(c)], dst, self.w_sem.at[0])
        out = lambda: self.remote(
            self.w.at[:, cols(other)], dst, self.w_sem.at[1], self.w_sem.at[2], self.dev(core=other)
        )
        return local, out

    def wait_weight(self):
        half = self.wv.at[:, pl.ds(0, self.shard)]
        for e in range(3):
            self.settle(half, self.w_sem.at[e])

    def grad_weight(self, lo, hi):
        c, other = self.core, 1 - self.core

        @pl.loop(lo, hi, unroll=BLOCKS)
        def _(j):
            self.gwb[j] = jnp.dot(self.dlt[...], self.hidden_block(j), preferred_element_type=F32).astype(BF16)
            src = lambda h: self.gwb.at[j, pl.ds(pl.multiple_of(h * self.shard, 16), self.shard)]
            dst = self.gw.at[:, pl.ds(pl.multiple_of(j * FULL + c * HALF, HALF), HALF)]
            pltpu.make_async_copy(src(c), dst, self.g_sem.at[0]).start()
            self.send(src(other), dst, self.g_sem.at[1], self.g_sem.at[2], self.dev(core=other))

    def run(self):
        other = 1 - self.core
        barrier = pltpu.get_barrier_semaphore()
        peers = [dict(x=dx, y=dy) for dx in range(4) for dy in range(4) if dx or dy]
        peers += [dict(z=dz) for dz in range(1, 8)]
        peers += [dict(core=other, z=dz) for dz in range(8)]
        for d in peers:
            pl.semaphore_signal(barrier, inc=1, device_id=self.dev(**d), device_id_type=MESH)
        for a in WIDE:
            self.spread_own(a).start()

        @pl.loop(0, NB)
        def _(j):
            self.weight_copies(j)[0].start()

        pl.semaphore_wait(barrier, len(peers))
        self.spread()
        self.spread_wait()
        self.gather()
        self.loss_and_grads()
        self.reduce()


def scratch(shard):
    dma = pltpu.SemaphoreType.DMA
    rows = 2 * shard
    out = {
        "wv": pltpu.VMEM((NB, rows, HALF), BF16),
        "lg": pltpu.VMEM((rows, 256), F32),
        "lg_in": pltpu.VMEM((rows, 256), F32),
        "lg_sum": pltpu.VMEM((rows, 256), F32),
        "st0": pltpu.VMEM((16, 8, 256), F32),
        "st1": pltpu.VMEM((8, 8, 256), F32),
        "dlt": pltpu.VMEM((rows, 256), BF16),
        "dlr": pltpu.VMEM((256, rows), BF16),
        "gwb": pltpu.VMEM((NB, rows, HALF), BF16),
        "ag_send": dma((NS, 2)),
        "ag_recv": dma((NS, 2, 2, 2, 4)),
        "rs_send": dma((NS, 2)),
        "rs_recv": dma((NS, 2, 2, 2, 4)),
        "lg_sem": dma((2,)),
        "st0_sem": dma((2,)),
        "st1_sem": dma((2,)),
        "w_sem": dma((3,)),
        "g_sem": dma((3,)),
    }
    for a in WIDE:
        n, width = SIZE[a], WIDE[a][1]
        out[f"first{a}"] = pltpu.VMEM((2, n, ROWS, width), BF16)
        out[f"first_sem{a}"] = dma((2,))
        out[f"last_out{a}"] = pltpu.VMEM((2, n, ROWS, width), F32)
        out[f"last_in{a}"] = pltpu.VMEM((2 * n, ROWS, width), F32)
        out[f"last_sem{a}"] = dma((2, 2))
    for i, (order, _, width) in enumerate(STREAMS):
        l, m, f = lead(order)
        out[f"buf{i}"] = pltpu.VMEM((l, m, f, 2 * ROWS, width), BF16)
        out[f"part{i}"] = pltpu.VMEM((l, m, f, 2 * ROWS, width), F32)
        chunk = {2: (m, f, 2 * ROWS, width), 1: (f, 2 * ROWS, width)}
        for p in (1, 2):
            shape = (2, hops(order, p)) + chunk[p]
            out[f"rs_out{i}{p}"] = pltpu.VMEM(shape, BF16)
            out[f"rs_in{i}{p}"] = pltpu.VMEM(shape, BF16)
    return out


def on_device(hidden, head_weight, targets, loss_weight):
    shard, width = head_weight.shape
    spaces = scratch(shard)

    def body(hid, w, tgt, lw, loss, gw, gh, *refs):
        named = dict(zip(spaces, refs))
        args = dict(hid=hid, w=w, tgt=tgt, lw=lw, loss=loss, gw=gw, gh=gh)
        for kind in ("buf", "part"):
            args[kind] = [named.pop(f"{kind}{i}") for i in range(NS)]
        for kind in ("rs_out", "rs_in"):
            args[kind] = [{p: named.pop(f"{kind}{i}{p}") for p in (1, 2)} for i in range(NS)]
        for kind in ("first", "first_sem", "last_out", "last_in", "last_sem"):
            args[kind] = {a: named.pop(f"{kind}{a}") for a in WIDE}
        args.update(named)
        Kernel(shard, args).run()

    vmem, hbm = pl.BlockSpec(memory_space=pltpu.VMEM), pl.BlockSpec(memory_space=pl.ANY)
    loss, gw, gh = pl.pallas_call(
        body,
        out_shape=(
            pltpu.VMEM(loss_weight.shape, F32),
            pltpu.VMEM((shard, width), BF16),
            pltpu.VMEM(hidden.shape, BF16),
        ),
        in_specs=[hbm, hbm, vmem, vmem],
        out_specs=(vmem, vmem, vmem),
        scratch_shapes=list(spaces.values()),
        compiler_params=pltpu.CompilerParams(
            collective_id=0, has_side_effects=True, vmem_limit_bytes=56 * 1024 * 1024
        ),
        cost_estimate=pl.CostEstimate(
            flops=6 * shard * width * 256, bytes_accessed=4 * shard * width, transcendentals=2 * shard * 512
        ),
    )(hidden, head_weight, targets, loss_weight)
    return (loss, gw, gh)


def solution(mesh):
    in_specs = (P("section", "tensor"), P(("section", "tensor"), None), P(), P())
    out_specs = (P(), P(("section", "tensor"), None), P("section", "tensor"))
    return jax.shard_map(
        on_device, mesh=mesh, in_specs=in_specs, out_specs=out_specs, check_vma=False
    )
```

```python
import math

import jax
import jax.numpy as jnp
from jax import lax
from jax.experimental import pallas as pl
from jax.experimental.pallas import tpu as pltpu
from jax.sharding import PartitionSpec as P

MESH = pl.DeviceIdType.MESH
F32, BF16 = jnp.float32, jnp.bfloat16
SIZE = {"x": 4, "y": 4, "z": 8, "a": 4, "b": 4}
ZH, ZL = 2, 4
NB = SIZE["y"] * ZL
NQ = ZH * SIZE["x"]
ROWS = 16
FULL, HALF = 1024, 512
STREAMS = (
    (("z", "b", "a"), 0, 128),
    (("z", "a", "b"), 128, 128),
    (("y", "x", "z"), 256, 256),
)
NS = len(STREAMS)
WIDE = {"z": (0, 256), "y": (256, 256)}
LONG = [i for i in range(NS) if STREAMS[i][0][2] == "z"]
SHORT = [i for i in range(NS) if i not in LONG]
BLOCKS = 2


def flat(ref, idx, count):
    dims = ref.shape[:-1]
    start, rows = 0, math.prod(dims[len(idx) :])
    for e, n in zip(idx, dims):
        start = start * n + e
    start = pl.multiple_of(start * rows, 32)
    return ref.reshape(math.prod(dims), ref.shape[-1]).at[pl.ds(start, count * rows)]


def lead(order):
    f, m, l = (SIZE[a] for a in order)
    return (l, m, f)


def hops(order, p):
    return SIZE[order[p]] // 2


class Kernel:
    def __init__(self, shard, refs):
        self.shard = shard
        self.__dict__.update(refs)
        sec, ten = lax.axis_index("section"), lax.axis_index("tensor")
        self.core = lax.rem(sec, 2)
        z = (sec // 8) * 4 + lax.rem(ten, 4)
        x, y = lax.rem(sec // 2, 4), ten // 4
        self.me = {"x": x, "y": y, "z": z} | self.roles(x, y)
        self.vocab0 = ((sec - self.core) * 16 + ten) * shard

    def roles(self, x, y):
        return {"a": jnp.where(self.core == 0, y, x), "b": jnp.where(self.core == 0, x, y)}

    def dev(self, core=None, **move):
        c = dict(self.me)
        for a, d in move.items():
            c[a] = lax.rem(c[a] + d + SIZE[a], SIZE[a])
            if a in ("a", "b"):
                first = self.core == (0 if a == "b" else 1)
                c["x"], c["y"] = jnp.where(first, c[a], c["x"]), jnp.where(first, c["y"], c[a])
        core = self.core if core is None else core
        return ((c["z"] // 4) * 8 + c["x"] * 2 + core, c["y"] * 4 + lax.rem(c["z"], 4))

    def remote(self, src, dst, ssem, rsem, device):
        return pltpu.make_async_remote_copy(
            src_ref=src, dst_ref=dst, send_sem=ssem, recv_sem=rsem, device_id=device, device_id_type=MESH
        )

    def send(self, *args):
        self.remote(*args).start()

    def settle(self, ref, sem):
        pltpu.make_async_copy(ref, ref, sem).wait()

    def spread_own(self, a):
        col, width = WIDE[a]
        src = self.hid.at[:, pl.ds(pl.multiple_of(self.core * HALF + col, 128), width)]
        return pltpu.make_async_copy(src, self.first[a].at[self.core, self.me[a]], self.first_sem[a].at[1])

    def spread(self):
        for a in ("z", "y"):
            n = SIZE[a]
            col, width = WIDE[a]

            @pl.loop(1, 2 * n)
            def _(e):
                to_core = lax.rem(self.core + e, 2)
                src = self.hid.at[:, pl.ds(pl.multiple_of(to_core * HALF + col, 128), width)]
                dst = self.first[a].at[self.core, self.me[a]]
                dev = self.dev(core=to_core, **{a: e // 2})
                self.send(src, dst, self.first_sem[a].at[0], self.first_sem[a].at[1], dev)

    def first_flat(self, a):
        return self.first[a].reshape(2 * SIZE[a], ROWS, WIDE[a][1])

    def spread_wait(self):
        for a in ("z", "y"):
            self.settle(self.first[a], self.first_sem[a].at[1])

    def settle_all(self, ref, sem, count):
        self.settle(ref.at[pl.ds(0, count)], sem)

    def gather_copy(self, i, p, way, kind, hop):
        order = STREAMS[i][0]
        a = order[p]
        n, w = SIZE[a], SIZE[order[p - 1]] // 2
        sign = 1 - 2 * way
        half = way if kind == 0 else 1 - way
        idx = (self.me[order[2]],) if p == 1 else ()
        out = lax.rem(self.me[a] - sign * (hop - 1) + n, n)
        got = lax.rem(self.me[a] - sign * hop + n, n)
        at = half * w
        sems = (self.ag_send.at[i, p - 1], self.ag_recv.at[i, p - 1, way, kind, hop - 1])
        dev = self.dev(**{a: sign})
        src, dst = (flat(self.buf[i], idx + (e, at), w) for e in (out, got))
        return (src, src) + sems + (dev,), (dst, dst) + sems + (dev,)

    def gather_event(self, i, p, s):
        h = hops(STREAMS[i][0], p)
        ways = [(kind, way) for kind in (0, 1) for way in (0, 1)]
        if s == h:
            for kind, way in ways:
                self.remote(*self.gather_copy(i, p, way, kind, h - kind)[1]).wait_recv()
            return
        for kind, way in ways:
            if s == 0:
                self.send(*self.gather_copy(i, p, way, kind, 1)[0])
            elif s < h - kind:
                self.remote(*self.gather_copy(i, p, way, kind, s)[1]).wait_recv()
                self.send(*self.gather_copy(i, p, way, kind, s + 1)[0])

    def reduce_copy(self, i, p, way, kind, hop):
        order = STREAMS[i][0]
        w = SIZE[order[p - 1]] // 2
        half = way if kind == 0 else 1 - way
        at = (way, hop - 1, half * w)
        return (
            flat(self.rs_out[i][p], at, w),
            flat(self.rs_in[i][p], at, w),
            self.rs_send.at[i, p - 1],
            self.rs_recv.at[i, p - 1, way, kind, hop - 1],
            self.dev(**{order[p]: 1 - 2 * way}),
        )

    def over(self, p, lo, size, body):
        if p == 2:
            for r in range(lo, lo + size):
                body((r,))
        else:
            body((pl.ds(lo, size),))

    def reduce_event(self, i, p, s):
        order = STREAMS[i][0]
        a = order[p]
        n, w, h = SIZE[a], SIZE[order[p - 1]] // 2, hops(order, p)
        part, out, got = self.part[i], self.rs_out[i][p], self.rs_in[i][p]
        base = (self.me[order[2]],) if p == 1 else ()
        ways = [(kind, way) for kind in (0, 1) for way in (0, 1)]
        if s == h:
            for kind, way in ways:
                self.remote(*self.reduce_copy(i, p, way, kind, h - kind)).wait_recv()
            mine = base + (self.me[a],)
            for half in (0, 1):
                far, near = (half, h - 1), (1 - half, h - 2)

                def add(r):
                    part[mine + r] = part[mine + r] + (got[far + r].astype(F32) + got[near + r].astype(F32))

                self.over(p, half * w, w, add)
            return
        for kind, way in ways:
            if s and s >= h - kind:
                continue
            if s:
                self.remote(*self.reduce_copy(i, p, way, kind, s)).wait_recv()
            half = way if kind == 0 else 1 - way
            d = h - kind - s
            idx = base + (lax.rem(self.me[a] + (1 - 2 * way) * d + n, n),)

            def put(r):
                v = part[idx + r]
                if s:
                    v = v + got[(way, s - 1) + r].astype(F32)
                out[(way, s) + r] = v.astype(BF16)

            self.over(p, half * w, w, put)
            self.send(*self.reduce_copy(i, p, way, kind, s + 1))

    def collect_copy(self, g, a, d):
        to = lax.rem(self.me[a] + d, SIZE[a])
        sem = self.last_sem[a]
        slot = self.last_in[a].at[self.me[a] * 2 + self.core]
        return self.remote(self.last_out[a].at[g, to], slot, sem.at[0, g], sem.at[1, 0], self.dev(core=g, **{a: d}))

    def collect_send(self, g, a):
        col = WIDE[a][0]
        out = self.last_out[a]
        for i in range(NS):
            order, off, width = STREAMS[i]
            if order[0] == a:
                mine = self.part[i].at[self.me[order[2]], self.me[order[1]]]
                out[g, :, :, off - col : off - col + width] = mine[:, g * ROWS : (g + 1) * ROWS]

        @pl.loop(1, SIZE[a])
        def _(d):
            self.collect_copy(g, a, d).start()

        @pl.when(self.core != g)
        def _():
            self.collect_copy(g, a, 0).start()

        @pl.when(self.core == g)
        def _():
            self.last_in[a][self.me[a] * 2 + g] = out[g, self.me[a]]

    def collect_wait(self, g, a):
        n = SIZE[a]
        col, width = WIDE[a]
        sem = self.last_sem[a]
        buf = self.last_in[a]

        @pl.when(self.core == g)
        def _():
            self.settle_all(self.last_out[a].at[g], sem.at[0, g], n - 1)
            self.settle_all(buf, sem.at[1, 0], 2 * n - 1)
            for c in (0, 1):
                v = buf[c]
                for e in range(1, n):
                    v = v + buf[2 * e + c]
                self.gh[:, c * HALF + col : c * HALF + col + width] = v.astype(BF16)

        @pl.when(self.core != g)
        def _():
            self.settle(self.last_out[a].at[g], sem.at[0, g])

    def piece(self, i, y, zl):
        order, _, _ = STREAMS[i]
        return jnp.concatenate([self.buf[i][self.at(order, x, y, zh * ZL + zl)] for zh in range(ZH) for x in range(4)], axis=0)

    def at(self, order, x, y, z):
        c = {"x": x, "y": y, "z": z} | self.roles(x, y)
        return (c[order[2]], c[order[1]], c[order[0]])

    def hidden_block(self, j):
        y, zl = j // ZL, lax.rem(j, ZL)
        return jnp.concatenate([self.piece(i, y, zl) for i in range(NS)], axis=1)

    def gather(self):
        for i, (order, off, width) in enumerate(STREAMS):
            col = off - WIDE[order[0]][0]
            mine = self.buf[i].at[self.me[order[2]], self.me[order[1]]]
            for g in (0, 1):
                mine[:, g * ROWS : (g + 1) * ROWS] = self.first[order[0]][g, :, :, col : col + width]
            self.gather_event(i, 1, 0)
        for i in range(NS):
            self.gather_event(i, 1, 1)
        for i in LONG + SHORT:
            self.gather_event(i, 1, 2)
            self.gather_event(i, 2, 0)

        @pl.loop(0, NB)
        def _(j):
            self.weight_copies(j)[1]().start()

        for streams, s in ((LONG, 1), (SHORT, 1), (LONG, 2), (LONG, 3), (SHORT, 2), (LONG, 4)):
            for i in streams:
                self.gather_event(i, 2, s)

    def settle_ring(self, sems, phases):
        for i, (order, _, _) in enumerate(STREAMS):
            for p in phases:
                ref = self.buf[i].at[0] if p == 1 else self.buf[i]
                self.settle_all(ref, sems.at[i, p - 1], SIZE[order[p]] - 1)

    def reduce(self):
        for i in LONG + SHORT:
            self.reduce_event(i, 2, 0)
        self.grad_weight(0, NB // 2)
        for i in LONG:
            self.reduce_event(i, 2, 1)
        for i in SHORT:
            self.reduce_event(i, 2, 1)
        for i in LONG:
            self.reduce_event(i, 2, 2)
        self.grad_weight(NB // 2, NB)
        for i in LONG:
            self.reduce_event(i, 2, 3)
        for a in ("z", "y"):
            self.settle_all(self.first_flat(a), self.first_sem[a].at[0], 2 * SIZE[a] - 1)
        self.settle_all(self.st0, self.st0_sem.at[0], 15)
        self.settle_all(self.st1, self.st1_sem.at[0], 7)
        self.settle(self.lg, self.lg_sem.at[0])
        self.settle_ring(self.ag_send, (1, 2))
        for i in SHORT:
            self.reduce_event(i, 2, 2)
            self.reduce_event(i, 1, 0)
        for i in LONG:
            self.reduce_event(i, 2, 4)
            self.reduce_event(i, 1, 0)
        for i in SHORT + LONG:
            self.reduce_event(i, 1, 1)
        for i in SHORT:
            self.reduce_event(i, 1, 2)
        for g in (0, 1):
            self.collect_send(g, "z")
        for i in LONG:
            self.reduce_event(i, 1, 2)
        for g in (0, 1):
            self.collect_send(g, "y")
        self.settle_ring(self.rs_send, (2, 1))
        half = self.gwb.at[:, pl.ds(0, self.shard)]
        for e in range(3):
            self.settle(half, self.g_sem.at[e])
        for a in ("z", "y"):
            for g in (0, 1):
                self.collect_wait(g, a)

    def loss_and_grads(self):
        self.wait_weight()
        acc = self.lg
        acc[...] = jnp.zeros_like(acc)

        @pl.loop(0, NB // BLOCKS)
        def _(b):
            js = [b * BLOCKS + e for e in range(BLOCKS)]
            acc[...] += lax.dot_general(
                jnp.concatenate([self.wv[j] for j in js], axis=1),
                jnp.concatenate([self.hidden_block(j) for j in js], axis=1),
                (((1,), (1,)), ((), ())),
                preferred_element_type=F32,
            )

        swap = (acc, self.lg_in, self.lg_sem.at[0], self.lg_sem.at[1], self.dev(core=1 - self.core))
        self.send(*swap)
        target, scale = self.tgt[...].reshape(1, -1), self.lw[...].reshape(1, -1)
        self.remote(*swap).wait_recv()
        logits = acc[...] + self.lg_in[...]
        self.lg_sum[...] = logits
        row = lax.broadcasted_iota(jnp.int32, logits.shape, 0)
        row = row + jnp.where(row < self.shard, self.vocab0, self.vocab0 + 15 * self.shard)
        hit = row == target
        top = jnp.max(logits, axis=0, keepdims=True)
        total = jnp.sum(jnp.exp(logits - top), axis=0, keepdims=True)
        picked = jnp.sum(jnp.where(hit, logits, 0.0), axis=0, keepdims=True)
        top, total, picked = self.stats(1, self.stats(0, (top, total, picked)))
        lse = top + jnp.log(total)
        self.loss[...] = (lse - picked).reshape(2 * NQ * ROWS)
        dl = scale * (jnp.exp(self.lg_sum[...] - lse) - (row == target).astype(F32))
        self.dlt[...] = dl.astype(BF16)
        self.dlr[...] = dl.T.astype(BF16)

        @pl.loop(0, NB, unroll=BLOCKS)
        def _(j):
            y, zl = j // ZL, lax.rem(j, ZL)
            o = jnp.dot(self.dlr[...], self.wv[j], preferred_element_type=F32)
            for i, (order, off, width) in enumerate(STREAMS):
                for zh in range(ZH):
                    for x in range(4):
                        q = (zh * 4 + x) * 2 * ROWS
                        self.part[i][self.at(order, x, y, zh * ZL + zl)] = o[q : q + 2 * ROWS, off : off + width]

    def stats(self, phase, mine):
        buf = (self.st0, self.st1)[phase]
        sem = (self.st0_sem, self.st1_sem)[phase]
        own = self.me["x"] * 4 + self.me["y"] if phase == 0 else self.me["z"]
        n = buf.shape[0]
        buf[own] = jnp.concatenate(mine + (jnp.zeros((5, 256), F32),), axis=0)

        @pl.loop(1, n)
        def _(e):
            dev = self.dev(x=e // 4, y=lax.rem(e, 4)) if phase == 0 else self.dev(z=e)
            self.send(buf.at[own], buf.at[own], sem.at[0], sem.at[1], dev)

        self.settle_all(buf, sem.at[1], n - 1)
        tiles = [buf[e] for e in range(n)]
        top = tiles[0][0:1]
        for t in tiles[1:]:
            top = jnp.maximum(top, t[0:1])
        total = picked = jnp.zeros_like(top)
        for t in tiles:
            total = total + t[1:2] * jnp.exp(t[0:1] - top)
            picked = picked + t[2:3]
        return (top, total, picked)

    def weight_copies(self, j):
        c, other = self.core, 1 - self.core
        rows = pl.ds(pl.multiple_of(c * self.shard, 16), self.shard)
        cols = lambda h: pl.ds(pl.multiple_of(j * FULL + h * HALF, HALF), HALF)
        dst = self.wv.at[j, rows]
        local = pltpu.make_async_copy(self.w.at[:, cols(c)], dst, self.w_sem.at[0])
        out = lambda: self.remote(
            self.w.at[:, cols(other)], dst, self.w_sem.at[1], self.w_sem.at[2], self.dev(core=other)
        )
        return local, out

    def wait_weight(self):
        half = self.wv.at[:, pl.ds(0, self.shard)]
        for e in range(3):
            self.settle(half, self.w_sem.at[e])

    def grad_weight(self, lo, hi):
        c, other = self.core, 1 - self.core

        @pl.loop(lo, hi, unroll=BLOCKS)
        def _(j):
            self.gwb[j] = jnp.dot(self.dlt[...], self.hidden_block(j), preferred_element_type=F32).astype(BF16)
            src = lambda h: self.gwb.at[j, pl.ds(pl.multiple_of(h * self.shard, 16), self.shard)]
            dst = self.gw.at[:, pl.ds(pl.multiple_of(j * FULL + c * HALF, HALF), HALF)]
            pltpu.make_async_copy(src(c), dst, self.g_sem.at[0]).start()
            self.send(src(other), dst, self.g_sem.at[1], self.g_sem.at[2], self.dev(core=other))

    def run(self):
        other = 1 - self.core
        barrier = pltpu.get_barrier_semaphore()
        peers = [dict(x=dx, y=dy) for dx in range(4) for dy in range(4) if dx or dy]
        peers += [dict(z=dz) for dz in range(1, 8)]
        peers += [dict(core=other, z=dz) for dz in range(8)]
        peers += [dict(core=other, y=dy) for dy in range(1, 4)]
        for d in peers:
            pl.semaphore_signal(barrier, inc=1, device_id=self.dev(**d), device_id_type=MESH)
        for a in ("z", "y"):
            self.spread_own(a).start()

        @pl.loop(0, NB)
        def _(j):
            self.weight_copies(j)[0].start()

        pl.semaphore_wait(barrier, len(peers))
        self.spread()
        self.spread_wait()
        self.gather()
        self.loss_and_grads()
        self.reduce()


def scratch(shard):
    dma = pltpu.SemaphoreType.DMA
    rows = 2 * shard
    out = {
        "wv": pltpu.VMEM((NB, rows, HALF), BF16),
        "lg": pltpu.VMEM((rows, 256), F32),
        "lg_in": pltpu.VMEM((rows, 256), F32),
        "lg_sum": pltpu.VMEM((rows, 256), F32),
        "st0": pltpu.VMEM((16, 8, 256), F32),
        "st1": pltpu.VMEM((8, 8, 256), F32),
        "dlt": pltpu.VMEM((rows, 256), BF16),
        "dlr": pltpu.VMEM((256, rows), BF16),
        "gwb": pltpu.VMEM((NB, rows, HALF), BF16),
        "ag_send": dma((NS, 2)),
        "ag_recv": dma((NS, 2, 2, 2, 4)),
        "rs_send": dma((NS, 2)),
        "rs_recv": dma((NS, 2, 2, 2, 4)),
        "lg_sem": dma((2,)),
        "st0_sem": dma((2,)),
        "st1_sem": dma((2,)),
        "w_sem": dma((3,)),
        "g_sem": dma((3,)),
    }
    for a in ("z", "y"):
        n, width = SIZE[a], WIDE[a][1]
        out[f"first{a}"] = pltpu.VMEM((2, n, ROWS, width), BF16)
        out[f"first_sem{a}"] = dma((2,))
        out[f"last_out{a}"] = pltpu.VMEM((2, n, ROWS, width), F32)
        out[f"last_in{a}"] = pltpu.VMEM((2 * n, ROWS, width), F32)
        out[f"last_sem{a}"] = dma((2, 2))
    for i, (order, _, width) in enumerate(STREAMS):
        l, m, f = lead(order)
        out[f"buf{i}"] = pltpu.VMEM((l, m, f, 2 * ROWS, width), BF16)
        out[f"part{i}"] = pltpu.VMEM((l, m, f, 2 * ROWS, width), F32)
        chunk = {2: (m, f, 2 * ROWS, width), 1: (f, 2 * ROWS, width)}
        for p in (1, 2):
            shape = (2, hops(order, p)) + chunk[p]
            out[f"rs_out{i}{p}"] = pltpu.VMEM(shape, BF16)
            out[f"rs_in{i}{p}"] = pltpu.VMEM(shape, BF16)
    return out


def on_device(hidden, head_weight, targets, loss_weight):
    shard, width = head_weight.shape
    spaces = scratch(shard)

    def body(hid, w, tgt, lw, loss, gw, gh, *refs):
        named = dict(zip(spaces, refs))
        args = dict(hid=hid, w=w, tgt=tgt, lw=lw, loss=loss, gw=gw, gh=gh)
        for kind in ("buf", "part"):
            args[kind] = [named.pop(f"{kind}{i}") for i in range(NS)]
        for kind in ("rs_out", "rs_in"):
            args[kind] = [{p: named.pop(f"{kind}{i}{p}") for p in (1, 2)} for i in range(NS)]
        for kind in ("first", "first_sem", "last_out", "last_in", "last_sem"):
            args[kind] = {a: named.pop(f"{kind}{a}") for a in ("z", "y")}
        args.update(named)
        Kernel(shard, args).run()

    vmem, hbm = pl.BlockSpec(memory_space=pltpu.VMEM), pl.BlockSpec(memory_space=pl.ANY)
    loss, gw, gh = pl.pallas_call(
        body,
        out_shape=(
            pltpu.VMEM(loss_weight.shape, F32),
            pltpu.VMEM((shard, width), BF16),
            pltpu.VMEM(hidden.shape, BF16),
        ),
        in_specs=[hbm, hbm, vmem, vmem],
        out_specs=(vmem, vmem, vmem),
        scratch_shapes=list(spaces.values()),
        compiler_params=pltpu.CompilerParams(
            collective_id=0, has_side_effects=True, vmem_limit_bytes=56 * 1024 * 1024
        ),
        cost_estimate=pl.CostEstimate(
            flops=6 * shard * width * 256, bytes_accessed=4 * shard * width, transcendentals=2 * shard * 512
        ),
    )(hidden, head_weight, targets, loss_weight)
    return (loss, gw, gh)


def solution(mesh):
    in_specs = (P("section", "tensor"), P(("section", "tensor"), None), P(), P())
    out_specs = (P(), P(("section", "tensor"), None), P("section", "tensor"))
    return jax.shard_map(
        on_device, mesh=mesh, in_specs=in_specs, out_specs=out_specs, check_vma=False
    )
```

```python
import math

import jax
import jax.numpy as jnp
from jax import lax
from jax.experimental import pallas as pl
from jax.experimental.pallas import tpu as pltpu
from jax.sharding import PartitionSpec as P

MESH = pl.DeviceIdType.MESH
F32, BF16 = jnp.float32, jnp.bfloat16
SIZE = {"x": 4, "y": 4, "z": 8, "a": 4, "b": 4}
ZH, ZL = 2, 4
NB = SIZE["y"] * ZL
NQ = ZH * SIZE["x"]
ROWS = 16
FULL, HALF = 1024, 512
STREAMS = (
    (("z", "b", "a"), 0, 256),
    (("z", "a", "b"), 256, 128),
    (("y", "x", "z"), 384, 128),
)
NS = len(STREAMS)
WIDE = {"z": (0, 384), "y": (384, 128)}
LONG = [i for i in range(NS) if STREAMS[i][0][2] == "z"]
SHORT = [i for i in range(NS) if i not in LONG]
BLOCKS = 2


def flat(ref, idx, count):
    dims = ref.shape[:-1]
    start, rows = 0, math.prod(dims[len(idx) :])
    for e, n in zip(idx, dims):
        start = start * n + e
    start = pl.multiple_of(start * rows, 32)
    return ref.reshape(math.prod(dims), ref.shape[-1]).at[pl.ds(start, count * rows)]


def lead(order):
    f, m, l = (SIZE[a] for a in order)
    return (l, m, f)


def hops(order, p):
    return SIZE[order[p]] // 2


class Kernel:
    def __init__(self, shard, refs):
        self.shard = shard
        self.__dict__.update(refs)
        sec, ten = lax.axis_index("section"), lax.axis_index("tensor")
        self.core = lax.rem(sec, 2)
        z = (sec // 8) * 4 + lax.rem(ten, 4)
        x, y = lax.rem(sec // 2, 4), ten // 4
        self.me = {"x": x, "y": y, "z": z} | self.roles(x, y)
        self.vocab0 = ((sec - self.core) * 16 + ten) * shard

    def roles(self, x, y):
        return {"a": jnp.where(self.core == 0, y, x), "b": jnp.where(self.core == 0, x, y)}

    def dev(self, core=None, **move):
        c = dict(self.me)
        for a, d in move.items():
            c[a] = lax.rem(c[a] + d + SIZE[a], SIZE[a])
            if a in ("a", "b"):
                first = self.core == (0 if a == "b" else 1)
                c["x"], c["y"] = jnp.where(first, c[a], c["x"]), jnp.where(first, c["y"], c[a])
        core = self.core if core is None else core
        return ((c["z"] // 4) * 8 + c["x"] * 2 + core, c["y"] * 4 + lax.rem(c["z"], 4))

    def remote(self, src, dst, ssem, rsem, device):
        return pltpu.make_async_remote_copy(
            src_ref=src, dst_ref=dst, send_sem=ssem, recv_sem=rsem, device_id=device, device_id_type=MESH
        )

    def send(self, *args):
        self.remote(*args).start()

    def settle(self, ref, sem):
        pltpu.make_async_copy(ref, ref, sem).wait()

    def spread_own(self, a):
        col, width = WIDE[a]
        src = self.hid.at[:, pl.ds(pl.multiple_of(self.core * HALF + col, 128), width)]
        return pltpu.make_async_copy(src, self.first[a].at[self.core, self.me[a]], self.first_sem[a].at[1])

    def spread(self):
        for a in ("z", "y"):
            n = SIZE[a]
            col, width = WIDE[a]

            @pl.loop(1, 2 * n)
            def _(e):
                to_core = lax.rem(self.core + e, 2)
                src = self.hid.at[:, pl.ds(pl.multiple_of(to_core * HALF + col, 128), width)]
                dst = self.first[a].at[self.core, self.me[a]]
                dev = self.dev(core=to_core, **{a: e // 2})
                self.send(src, dst, self.first_sem[a].at[0], self.first_sem[a].at[1], dev)

    def first_flat(self, a):
        return self.first[a].reshape(2 * SIZE[a], ROWS, WIDE[a][1])

    def spread_wait(self):
        for a in ("z", "y"):
            self.settle(self.first[a], self.first_sem[a].at[1])

    def settle_all(self, ref, sem, count):
        self.settle(ref.at[pl.ds(0, count)], sem)

    def gather_copy(self, i, p, way, kind, hop):
        order = STREAMS[i][0]
        a = order[p]
        n, w = SIZE[a], SIZE[order[p - 1]] // 2
        sign = 1 - 2 * way
        half = way if kind == 0 else 1 - way
        idx = (self.me[order[2]],) if p == 1 else ()
        out = lax.rem(self.me[a] - sign * (hop - 1) + n, n)
        got = lax.rem(self.me[a] - sign * hop + n, n)
        at = half * w
        sems = (self.ag_send.at[i, p - 1], self.ag_recv.at[i, p - 1, way, kind, hop - 1])
        dev = self.dev(**{a: sign})
        src, dst = (flat(self.buf[i], idx + (e, at), w) for e in (out, got))
        return (src, src) + sems + (dev,), (dst, dst) + sems + (dev,)

    def gather_event(self, i, p, s):
        h = hops(STREAMS[i][0], p)
        ways = [(kind, way) for kind in (0, 1) for way in (0, 1)]
        if s == h:
            for kind, way in ways:
                self.remote(*self.gather_copy(i, p, way, kind, h - kind)[1]).wait_recv()
            return
        for kind, way in ways:
            if s == 0:
                self.send(*self.gather_copy(i, p, way, kind, 1)[0])
            elif s < h - kind:
                self.remote(*self.gather_copy(i, p, way, kind, s)[1]).wait_recv()
                self.send(*self.gather_copy(i, p, way, kind, s + 1)[0])

    def reduce_copy(self, i, p, way, kind, hop):
        order = STREAMS[i][0]
        w = SIZE[order[p - 1]] // 2
        half = way if kind == 0 else 1 - way
        at = (way, hop - 1, half * w)
        return (
            flat(self.rs_out[i][p], at, w),
            flat(self.rs_in[i][p], at, w),
            self.rs_send.at[i, p - 1],
            self.rs_recv.at[i, p - 1, way, kind, hop - 1],
            self.dev(**{order[p]: 1 - 2 * way}),
        )

    def over(self, p, lo, size, body):
        if p == 2:
            for r in range(lo, lo + size):
                body((r,))
        else:
            body((pl.ds(lo, size),))

    def reduce_event(self, i, p, s):
        order = STREAMS[i][0]
        a = order[p]
        n, w, h = SIZE[a], SIZE[order[p - 1]] // 2, hops(order, p)
        part, out, got = self.part[i], self.rs_out[i][p], self.rs_in[i][p]
        base = (self.me[order[2]],) if p == 1 else ()
        ways = [(kind, way) for kind in (0, 1) for way in (0, 1)]
        if s == h:
            for kind, way in ways:
                self.remote(*self.reduce_copy(i, p, way, kind, h - kind)).wait_recv()
            mine = base + (self.me[a],)
            for half in (0, 1):
                far, near = (half, h - 1), (1 - half, h - 2)

                def add(r):
                    part[mine + r] = part[mine + r] + (got[far + r].astype(F32) + got[near + r].astype(F32))

                self.over(p, half * w, w, add)
            return
        for kind, way in ways:
            if s and s >= h - kind:
                continue
            if s:
                self.remote(*self.reduce_copy(i, p, way, kind, s)).wait_recv()
            half = way if kind == 0 else 1 - way
            d = h - kind - s
            idx = base + (lax.rem(self.me[a] + (1 - 2 * way) * d + n, n),)

            def put(r):
                v = part[idx + r]
                if s:
                    v = v + got[(way, s - 1) + r].astype(F32)
                out[(way, s) + r] = v.astype(BF16)

            self.over(p, half * w, w, put)
            self.send(*self.reduce_copy(i, p, way, kind, s + 1))

    def collect_copy(self, g, a, d):
        to = lax.rem(self.me[a] + d, SIZE[a])
        sem = self.last_sem[a]
        slot = self.last_in[a].at[self.me[a] * 2 + self.core]
        return self.remote(self.last_out[a].at[g, to], slot, sem.at[0, g], sem.at[1, 0], self.dev(core=g, **{a: d}))

    def collect_send(self, g, a):
        col = WIDE[a][0]
        out = self.last_out[a]
        for i in range(NS):
            order, off, width = STREAMS[i]
            if order[0] == a:
                mine = self.part[i].at[self.me[order[2]], self.me[order[1]]]
                out[g, :, :, off - col : off - col + width] = mine[:, g * ROWS : (g + 1) * ROWS]

        @pl.loop(1, SIZE[a])
        def _(d):
            self.collect_copy(g, a, d).start()

        @pl.when(self.core != g)
        def _():
            self.collect_copy(g, a, 0).start()

        @pl.when(self.core == g)
        def _():
            self.last_in[a][self.me[a] * 2 + g] = out[g, self.me[a]]

    def collect_wait(self, g, a):
        n = SIZE[a]
        col, width = WIDE[a]
        sem = self.last_sem[a]
        buf = self.last_in[a]

        @pl.when(self.core == g)
        def _():
            self.settle_all(self.last_out[a].at[g], sem.at[0, g], n - 1)
            self.settle_all(buf, sem.at[1, 0], 2 * n - 1)
            for c in (0, 1):
                v = buf[c]
                for e in range(1, n):
                    v = v + buf[2 * e + c]
                self.gh[:, c * HALF + col : c * HALF + col + width] = v.astype(BF16)

        @pl.when(self.core != g)
        def _():
            self.settle(self.last_out[a].at[g], sem.at[0, g])

    def piece(self, i, y, zl):
        order, _, _ = STREAMS[i]
        return jnp.concatenate([self.buf[i][self.at(order, x, y, zh * ZL + zl)] for zh in range(ZH) for x in range(4)], axis=0)

    def at(self, order, x, y, z):
        c = {"x": x, "y": y, "z": z} | self.roles(x, y)
        return (c[order[2]], c[order[1]], c[order[0]])

    def hidden_block(self, j):
        y, zl = j // ZL, lax.rem(j, ZL)
        return jnp.concatenate([self.piece(i, y, zl) for i in range(NS)], axis=1)

    def gather(self):
        for i, (order, off, width) in enumerate(STREAMS):
            col = off - WIDE[order[0]][0]
            mine = self.buf[i].at[self.me[order[2]], self.me[order[1]]]
            for g in (0, 1):
                mine[:, g * ROWS : (g + 1) * ROWS] = self.first[order[0]][g, :, :, col : col + width]
            self.gather_event(i, 1, 0)
        for i in range(NS):
            self.gather_event(i, 1, 1)
        for i in SHORT + LONG:
            self.gather_event(i, 1, 2)
            self.gather_event(i, 2, 0)

        @pl.loop(0, NB)
        def _(j):
            self.weight_copies(j)[1]().start()

        for streams, s in ((LONG, 1), (SHORT, 1), (LONG, 2), (LONG, 3), (SHORT, 2), (LONG, 4)):
            for i in streams:
                self.gather_event(i, 2, s)

    def settle_ring(self, sems, phases):
        for i, (order, _, _) in enumerate(STREAMS):
            for p in phases:
                ref = self.buf[i].at[0] if p == 1 else self.buf[i]
                self.settle_all(ref, sems.at[i, p - 1], SIZE[order[p]] - 1)

    def reduce(self):
        quarter = NB // 4
        for i in SHORT + LONG:
            self.reduce_event(i, 2, 0)
        for i in LONG:
            self.reduce_event(i, 2, 1)
        self.grad_weight(0, quarter)
        for i in SHORT:
            self.reduce_event(i, 2, 1)
        for i in LONG:
            self.reduce_event(i, 2, 2)
        self.grad_weight(quarter, 2 * quarter)
        for i in LONG:
            self.reduce_event(i, 2, 3)
        self.grad_weight(2 * quarter, NB)
        for a in ("z", "y"):
            self.settle_all(self.first_flat(a), self.first_sem[a].at[0], 2 * SIZE[a] - 1)
        self.settle_all(self.st0, self.st0_sem.at[0], 15)
        self.settle_all(self.st1, self.st1_sem.at[0], 7)
        self.settle(self.lg, self.lg_sem.at[0])
        self.settle_ring(self.ag_send, (1, 2))
        for i in SHORT:
            self.reduce_event(i, 2, 2)
            self.reduce_event(i, 1, 0)
        for i in LONG:
            self.reduce_event(i, 2, 4)
            self.reduce_event(i, 1, 0)
        for i in SHORT + LONG:
            self.reduce_event(i, 1, 1)
        for i in SHORT:
            self.reduce_event(i, 1, 2)
        for g in (0, 1):
            self.collect_send(g, "z")
        for i in LONG:
            self.reduce_event(i, 1, 2)
        for g in (0, 1):
            self.collect_send(g, "y")
        self.settle_ring(self.rs_send, (2, 1))
        half = self.gwb.at[:, pl.ds(0, self.shard)]
        for e in range(3):
            self.settle(half, self.g_sem.at[e])
        for a in ("z", "y"):
            for g in (0, 1):
                self.collect_wait(g, a)

    def loss_and_grads(self):
        self.wait_weight()
        acc = self.lg
        acc[...] = jnp.zeros_like(acc)

        @pl.loop(0, NB // BLOCKS)
        def _(b):
            js = [b * BLOCKS + e for e in range(BLOCKS)]
            acc[...] += lax.dot_general(
                jnp.concatenate([self.wv[j] for j in js], axis=1),
                jnp.concatenate([self.hidden_block(j) for j in js], axis=1),
                (((1,), (1,)), ((), ())),
                preferred_element_type=F32,
            )

        swap = (acc, self.lg_in, self.lg_sem.at[0], self.lg_sem.at[1], self.dev(core=1 - self.core))
        self.send(*swap)
        target, scale = self.tgt[...].reshape(1, -1), self.lw[...].reshape(1, -1)
        self.remote(*swap).wait_recv()
        logits = acc[...] + self.lg_in[...]
        self.lg_sum[...] = logits
        row = lax.broadcasted_iota(jnp.int32, logits.shape, 0)
        row = row + jnp.where(row < self.shard, self.vocab0, self.vocab0 + 15 * self.shard)
        hit = row == target
        top = jnp.max(logits, axis=0, keepdims=True)
        total = jnp.sum(jnp.exp(logits - top), axis=0, keepdims=True)
        picked = jnp.sum(jnp.where(hit, logits, 0.0), axis=0, keepdims=True)
        top, total, picked = self.stats(1, self.stats(0, (top, total, picked)))
        lse = top + jnp.log(total)
        self.loss[...] = (lse - picked).reshape(2 * NQ * ROWS)
        dl = scale * (jnp.exp(self.lg_sum[...] - lse) - (row == target).astype(F32))
        self.dlt[...] = dl.astype(BF16)
        self.dlr[...] = dl.T.astype(BF16)

        @pl.loop(0, NB, unroll=BLOCKS)
        def _(j):
            y, zl = j // ZL, lax.rem(j, ZL)
            o = jnp.dot(self.dlr[...], self.wv[j], preferred_element_type=F32)
            for i, (order, off, width) in enumerate(STREAMS):
                for zh in range(ZH):
                    for x in range(4):
                        q = (zh * 4 + x) * 2 * ROWS
                        self.part[i][self.at(order, x, y, zh * ZL + zl)] = o[q : q + 2 * ROWS, off : off + width]

    def stats(self, phase, mine):
        buf = (self.st0, self.st1)[phase]
        sem = (self.st0_sem, self.st1_sem)[phase]
        own = self.me["x"] * 4 + self.me["y"] if phase == 0 else self.me["z"]
        n = buf.shape[0]
        buf[own] = jnp.concatenate(mine + (jnp.zeros((5, 256), F32),), axis=0)

        @pl.loop(1, n)
        def _(e):
            dev = self.dev(x=e // 4, y=lax.rem(e, 4)) if phase == 0 else self.dev(z=e)
            self.send(buf.at[own], buf.at[own], sem.at[0], sem.at[1], dev)

        self.settle_all(buf, sem.at[1], n - 1)
        tiles = [buf[e] for e in range(n)]
        top = tiles[0][0:1]
        for t in tiles[1:]:
            top = jnp.maximum(top, t[0:1])
        total = picked = jnp.zeros_like(top)
        for t in tiles:
            total = total + t[1:2] * jnp.exp(t[0:1] - top)
            picked = picked + t[2:3]
        return (top, total, picked)

    def weight_copies(self, j):
        c, other = self.core, 1 - self.core
        rows = pl.ds(pl.multiple_of(c * self.shard, 16), self.shard)
        cols = lambda h: pl.ds(pl.multiple_of(j * FULL + h * HALF, HALF), HALF)
        dst = self.wv.at[j, rows]
        local = pltpu.make_async_copy(self.w.at[:, cols(c)], dst, self.w_sem.at[0])
        out = lambda: self.remote(
            self.w.at[:, cols(other)], dst, self.w_sem.at[1], self.w_sem.at[2], self.dev(core=other)
        )
        return local, out

    def wait_weight(self):
        half = self.wv.at[:, pl.ds(0, self.shard)]
        for e in range(3):
            self.settle(half, self.w_sem.at[e])

    def grad_weight(self, lo, hi):
        c, other = self.core, 1 - self.core

        @pl.loop(lo, hi, unroll=BLOCKS)
        def _(j):
            self.gwb[j] = jnp.dot(self.dlt[...], self.hidden_block(j), preferred_element_type=F32).astype(BF16)
            src = lambda h: self.gwb.at[j, pl.ds(pl.multiple_of(h * self.shard, 16), self.shard)]
            dst = self.gw.at[:, pl.ds(pl.multiple_of(j * FULL + c * HALF, HALF), HALF)]
            pltpu.make_async_copy(src(c), dst, self.g_sem.at[0]).start()
            self.send(src(other), dst, self.g_sem.at[1], self.g_sem.at[2], self.dev(core=other))

    def run(self):
        other = 1 - self.core
        barrier = pltpu.get_barrier_semaphore()
        peers = [dict(x=dx, y=dy) for dx in range(4) for dy in range(4) if dx or dy]
        peers += [dict(z=dz) for dz in range(1, 8)]
        peers += [dict(core=other, z=dz) for dz in range(8)]
        peers += [dict(core=other, y=dy) for dy in range(1, 4)]
        for d in peers:
            pl.semaphore_signal(barrier, inc=1, device_id=self.dev(**d), device_id_type=MESH)
        for a in ("z", "y"):
            self.spread_own(a).start()

        @pl.loop(0, NB)
        def _(j):
            self.weight_copies(j)[0].start()

        pl.semaphore_wait(barrier, len(peers))
        self.spread()
        self.spread_wait()
        self.gather()
        self.loss_and_grads()
        self.reduce()


def scratch(shard):
    dma = pltpu.SemaphoreType.DMA
    rows = 2 * shard
    out = {
        "wv": pltpu.VMEM((NB, rows, HALF), BF16),
        "lg": pltpu.VMEM((rows, 256), F32),
        "lg_in": pltpu.VMEM((rows, 256), F32),
        "lg_sum": pltpu.VMEM((rows, 256), F32),
        "st0": pltpu.VMEM((16, 8, 256), F32),
        "st1": pltpu.VMEM((8, 8, 256), F32),
        "dlt": pltpu.VMEM((rows, 256), BF16),
        "dlr": pltpu.VMEM((256, rows), BF16),
        "gwb": pltpu.VMEM((NB, rows, HALF), BF16),
        "ag_send": dma((NS, 2)),
        "ag_recv": dma((NS, 2, 2, 2, 4)),
        "rs_send": dma((NS, 2)),
        "rs_recv": dma((NS, 2, 2, 2, 4)),
        "lg_sem": dma((2,)),
        "st0_sem": dma((2,)),
        "st1_sem": dma((2,)),
        "w_sem": dma((3,)),
        "g_sem": dma((3,)),
    }
    for a in ("z", "y"):
        n, width = SIZE[a], WIDE[a][1]
        out[f"first{a}"] = pltpu.VMEM((2, n, ROWS, width), BF16)
        out[f"first_sem{a}"] = dma((2,))
        out[f"last_out{a}"] = pltpu.VMEM((2, n, ROWS, width), F32)
        out[f"last_in{a}"] = pltpu.VMEM((2 * n, ROWS, width), F32)
        out[f"last_sem{a}"] = dma((2, 2))
    for i, (order, _, width) in enumerate(STREAMS):
        l, m, f = lead(order)
        out[f"buf{i}"] = pltpu.VMEM((l, m, f, 2 * ROWS, width), BF16)
        out[f"part{i}"] = pltpu.VMEM((l, m, f, 2 * ROWS, width), F32)
        chunk = {2: (m, f, 2 * ROWS, width), 1: (f, 2 * ROWS, width)}
        for p in (1, 2):
            shape = (2, hops(order, p)) + chunk[p]
            out[f"rs_out{i}{p}"] = pltpu.VMEM(shape, BF16)
            out[f"rs_in{i}{p}"] = pltpu.VMEM(shape, BF16)
    return out


def on_device(hidden, head_weight, targets, loss_weight):
    shard, width = head_weight.shape
    spaces = scratch(shard)

    def body(hid, w, tgt, lw, loss, gw, gh, *refs):
        named = dict(zip(spaces, refs))
        args = dict(hid=hid, w=w, tgt=tgt, lw=lw, loss=loss, gw=gw, gh=gh)
        for kind in ("buf", "part"):
            args[kind] = [named.pop(f"{kind}{i}") for i in range(NS)]
        for kind in ("rs_out", "rs_in"):
            args[kind] = [{p: named.pop(f"{kind}{i}{p}") for p in (1, 2)} for i in range(NS)]
        for kind in ("first", "first_sem", "last_out", "last_in", "last_sem"):
            args[kind] = {a: named.pop(f"{kind}{a}") for a in ("z", "y")}
        args.update(named)
        Kernel(shard, args).run()

    vmem, hbm = pl.BlockSpec(memory_space=pltpu.VMEM), pl.BlockSpec(memory_space=pl.ANY)
    loss, gw, gh = pl.pallas_call(
        body,
        out_shape=(
            pltpu.VMEM(loss_weight.shape, F32),
            pltpu.VMEM((shard, width), BF16),
            pltpu.VMEM(hidden.shape, BF16),
        ),
        in_specs=[hbm, hbm, vmem, vmem],
        out_specs=(vmem, vmem, vmem),
        scratch_shapes=list(spaces.values()),
        compiler_params=pltpu.CompilerParams(
            collective_id=0, has_side_effects=True, vmem_limit_bytes=56 * 1024 * 1024
        ),
        cost_estimate=pl.CostEstimate(
            flops=6 * shard * width * 256, bytes_accessed=4 * shard * width, transcendentals=2 * shard * 512
        ),
    )(hidden, head_weight, targets, loss_weight)
    return (loss, gw, gh)


def solution(mesh):
    in_specs = (P("section", "tensor"), P(("section", "tensor"), None), P(), P())
    out_specs = (P(), P(("section", "tensor"), None), P("section", "tensor"))
    return jax.shard_map(
        on_device, mesh=mesh, in_specs=in_specs, out_specs=out_specs, check_vma=False
    )
```

```python
import math

import jax
import jax.numpy as jnp
from jax import lax
from jax.experimental import pallas as pl
from jax.experimental.pallas import tpu as pltpu
from jax.sharding import PartitionSpec as P

MESH = pl.DeviceIdType.MESH
F32, BF16 = jnp.float32, jnp.bfloat16
SIZE = {"x": 4, "y": 4, "z": 8, "a": 4, "b": 4}
ZH, ZL = 2, 4
NB = SIZE["y"] * ZL
NQ = ZH * SIZE["x"]
ROWS = 16
FULL, HALF = 1024, 512
STREAMS = (
    (("z", "b", "a"), 0, 256),
    (("z", "a", "b"), 256, 128),
    (("y", "x", "z"), 384, 128),
)
NS = len(STREAMS)
WIDE = {"z": (0, 384), "y": (384, 128)}
LONG = [i for i in range(NS) if STREAMS[i][0][2] == "z"]
SHORT = [i for i in range(NS) if i not in LONG]
BLOCKS = 2


def flat(ref, idx, count):
    dims = ref.shape[:-1]
    start, rows = 0, math.prod(dims[len(idx) :])
    for e, n in zip(idx, dims):
        start = start * n + e
    start = pl.multiple_of(start * rows, 32)
    return ref.reshape(math.prod(dims), ref.shape[-1]).at[pl.ds(start, count * rows)]


def lead(order):
    f, m, l = (SIZE[a] for a in order)
    return (l, m, f)


def hops(order, p):
    return SIZE[order[p]] // 2


class Kernel:
    def __init__(self, shard, refs):
        self.shard = shard
        self.__dict__.update(refs)
        sec, ten = lax.axis_index("section"), lax.axis_index("tensor")
        self.core = lax.rem(sec, 2)
        z = (sec // 8) * 4 + lax.rem(ten, 4)
        x, y = lax.rem(sec // 2, 4), ten // 4
        self.me = {"x": x, "y": y, "z": z} | self.roles(x, y)
        self.vocab0 = ((sec - self.core) * 16 + ten) * shard

    def roles(self, x, y):
        return {"a": jnp.where(self.core == 0, y, x), "b": jnp.where(self.core == 0, x, y)}

    def dev(self, core=None, **move):
        c = dict(self.me)
        for a, d in move.items():
            c[a] = lax.rem(c[a] + d + SIZE[a], SIZE[a])
            if a in ("a", "b"):
                first = self.core == (0 if a == "b" else 1)
                c["x"], c["y"] = jnp.where(first, c[a], c["x"]), jnp.where(first, c["y"], c[a])
        core = self.core if core is None else core
        return ((c["z"] // 4) * 8 + c["x"] * 2 + core, c["y"] * 4 + lax.rem(c["z"], 4))

    def remote(self, src, dst, ssem, rsem, device):
        return pltpu.make_async_remote_copy(
            src_ref=src, dst_ref=dst, send_sem=ssem, recv_sem=rsem, device_id=device, device_id_type=MESH
        )

    def send(self, *args):
        self.remote(*args).start()

    def settle(self, ref, sem):
        pltpu.make_async_copy(ref, ref, sem).wait()

    def spread_own(self, a):
        col, width = WIDE[a]
        src = self.hid.at[:, pl.ds(pl.multiple_of(self.core * HALF + col, 128), width)]
        return pltpu.make_async_copy(src, self.first[a].at[self.core, self.me[a]], self.first_sem[a].at[1])

    def spread(self):
        for a in ("z", "y"):
            n = SIZE[a]
            col, width = WIDE[a]

            @pl.loop(1, 2 * n)
            def _(e):
                to_core = lax.rem(self.core + e, 2)
                src = self.hid.at[:, pl.ds(pl.multiple_of(to_core * HALF + col, 128), width)]
                dst = self.first[a].at[self.core, self.me[a]]
                dev = self.dev(core=to_core, **{a: e // 2})
                self.send(src, dst, self.first_sem[a].at[0], self.first_sem[a].at[1], dev)

    def first_flat(self, a):
        return self.first[a].reshape(2 * SIZE[a], ROWS, WIDE[a][1])

    def spread_wait(self):
        for a in ("z", "y"):
            self.settle(self.first[a], self.first_sem[a].at[1])

    def settle_all(self, ref, sem, count):
        self.settle(ref.at[pl.ds(0, count)], sem)

    def gather_copy(self, i, p, way, kind, hop):
        order = STREAMS[i][0]
        a = order[p]
        n, w = SIZE[a], SIZE[order[p - 1]] // 2
        sign = 1 - 2 * way
        half = way if kind == 0 else 1 - way
        idx = (self.me[order[2]],) if p == 1 else ()
        out = lax.rem(self.me[a] - sign * (hop - 1) + n, n)
        got = lax.rem(self.me[a] - sign * hop + n, n)
        at = half * w
        sems = (self.ag_send.at[i, p - 1], self.ag_recv.at[i, p - 1, way, kind, hop - 1])
        dev = self.dev(**{a: sign})
        src, dst = (flat(self.buf[i], idx + (e, at), w) for e in (out, got))
        return (src, src) + sems + (dev,), (dst, dst) + sems + (dev,)

    def gather_event(self, i, p, s):
        h = hops(STREAMS[i][0], p)
        ways = [(kind, way) for kind in (0, 1) for way in (0, 1)]
        if s == h:
            for kind, way in ways:
                self.remote(*self.gather_copy(i, p, way, kind, h - kind)[1]).wait_recv()
            return
        for kind, way in ways:
            if s == 0:
                self.send(*self.gather_copy(i, p, way, kind, 1)[0])
            elif s < h - kind:
                self.remote(*self.gather_copy(i, p, way, kind, s)[1]).wait_recv()
                self.send(*self.gather_copy(i, p, way, kind, s + 1)[0])

    def reduce_copy(self, i, p, way, kind, hop):
        order = STREAMS[i][0]
        w = SIZE[order[p - 1]] // 2
        half = way if kind == 0 else 1 - way
        at = (way, hop - 1, half * w)
        return (
            flat(self.rs_out[i][p], at, w),
            flat(self.rs_in[i][p], at, w),
            self.rs_send.at[i, p - 1],
            self.rs_recv.at[i, p - 1, way, kind, hop - 1],
            self.dev(**{order[p]: 1 - 2 * way}),
        )

    def over(self, p, lo, size, body):
        if p == 2:
            for r in range(lo, lo + size):
                body((r,))
        else:
            body((pl.ds(lo, size),))

    def reduce_event(self, i, p, s):
        order = STREAMS[i][0]
        a = order[p]
        n, w, h = SIZE[a], SIZE[order[p - 1]] // 2, hops(order, p)
        part, out, got = self.part[i], self.rs_out[i][p], self.rs_in[i][p]
        base = (self.me[order[2]],) if p == 1 else ()
        ways = [(kind, way) for kind in (0, 1) for way in (0, 1)]
        if s == h:
            for kind, way in ways:
                self.remote(*self.reduce_copy(i, p, way, kind, h - kind)).wait_recv()
            mine = base + (self.me[a],)
            for half in (0, 1):
                far, near = (half, h - 1), (1 - half, h - 2)

                def add(r):
                    part[mine + r] = part[mine + r] + (got[far + r].astype(F32) + got[near + r].astype(F32))

                self.over(p, half * w, w, add)
            return
        for kind, way in ways:
            if s and s >= h - kind:
                continue
            if s:
                self.remote(*self.reduce_copy(i, p, way, kind, s)).wait_recv()
            half = way if kind == 0 else 1 - way
            d = h - kind - s
            idx = base + (lax.rem(self.me[a] + (1 - 2 * way) * d + n, n),)

            def put(r):
                v = part[idx + r]
                if s:
                    v = v + got[(way, s - 1) + r].astype(F32)
                out[(way, s) + r] = v.astype(BF16)

            self.over(p, half * w, w, put)
            self.send(*self.reduce_copy(i, p, way, kind, s + 1))

    def collect_copy(self, g, a, d):
        to = lax.rem(self.me[a] + d, SIZE[a])
        sem = self.last_sem[a]
        slot = self.last_in[a].at[self.me[a] * 2 + self.core]
        return self.remote(self.last_out[a].at[g, to], slot, sem.at[0, g], sem.at[1, 0], self.dev(core=g, **{a: d}))

    def collect_send(self, g, a):
        col = WIDE[a][0]
        out = self.last_out[a]
        for i in range(NS):
            order, off, width = STREAMS[i]
            if order[0] == a:
                mine = self.part[i].at[self.me[order[2]], self.me[order[1]]]
                out[g, :, :, off - col : off - col + width] = mine[:, g * ROWS : (g + 1) * ROWS]

        @pl.loop(1, SIZE[a])
        def _(d):
            self.collect_copy(g, a, d).start()

        @pl.when(self.core != g)
        def _():
            self.collect_copy(g, a, 0).start()

        @pl.when(self.core == g)
        def _():
            self.last_in[a][self.me[a] * 2 + g] = out[g, self.me[a]]

    def collect_wait(self, g, a):
        n = SIZE[a]
        col, width = WIDE[a]
        sem = self.last_sem[a]
        buf = self.last_in[a]

        @pl.when(self.core == g)
        def _():
            self.settle_all(self.last_out[a].at[g], sem.at[0, g], n - 1)
            self.settle_all(buf, sem.at[1, 0], 2 * n - 1)
            for c in (0, 1):
                v = buf[c]
                for e in range(1, n):
                    v = v + buf[2 * e + c]
                self.gh[:, c * HALF + col : c * HALF + col + width] = v.astype(BF16)

        @pl.when(self.core != g)
        def _():
            self.settle(self.last_out[a].at[g], sem.at[0, g])

    def piece(self, i, y, zl):
        order, _, _ = STREAMS[i]
        return jnp.concatenate([self.buf[i][self.at(order, x, y, zh * ZL + zl)] for zh in range(ZH) for x in range(4)], axis=0)

    def at(self, order, x, y, z):
        c = {"x": x, "y": y, "z": z} | self.roles(x, y)
        return (c[order[2]], c[order[1]], c[order[0]])

    def hidden_block(self, j):
        y, zl = j // ZL, lax.rem(j, ZL)
        return jnp.concatenate([self.piece(i, y, zl) for i in range(NS)], axis=1)

    def gather(self):
        for i, (order, off, width) in enumerate(STREAMS):
            col = off - WIDE[order[0]][0]
            mine = self.buf[i].at[self.me[order[2]], self.me[order[1]]]
            for g in (0, 1):
                mine[:, g * ROWS : (g + 1) * ROWS] = self.first[order[0]][g, :, :, col : col + width]
            self.gather_event(i, 1, 0)
        for i in range(NS):
            self.gather_event(i, 1, 1)
        for i in SHORT + LONG:
            self.gather_event(i, 1, 2)
            self.gather_event(i, 2, 0)
        for streams, s in ((LONG, 1), (SHORT, 1), (LONG, 2), (LONG, 3), (SHORT, 2), (LONG, 4)):
            for i in streams:
                self.gather_event(i, 2, s)
            if streams is SHORT and s == 1:

                @pl.loop(0, NB)
                def _(j):
                    self.weight_copies(j)[1]().start()


    def settle_ring(self, sems, phases):
        for i, (order, _, _) in enumerate(STREAMS):
            for p in phases:
                ref = self.buf[i].at[0] if p == 1 else self.buf[i]
                self.settle_all(ref, sems.at[i, p - 1], SIZE[order[p]] - 1)

    def reduce(self):
        quarter = NB // 4
        for i in SHORT + LONG:
            self.reduce_event(i, 2, 0)
        for i in LONG:
            self.reduce_event(i, 2, 1)
        self.grad_weight(0, quarter)
        for i in SHORT:
            self.reduce_event(i, 2, 1)
        for i in LONG:
            self.reduce_event(i, 2, 2)
        self.grad_weight(quarter, 2 * quarter)
        for i in LONG:
            self.reduce_event(i, 2, 3)
        self.grad_weight(2 * quarter, NB)
        for a in ("z", "y"):
            self.settle_all(self.first_flat(a), self.first_sem[a].at[0], 2 * SIZE[a] - 1)
        self.settle_all(self.st0, self.st0_sem.at[0], 15)
        self.settle_all(self.st1, self.st1_sem.at[0], 7)
        self.settle(self.lg, self.lg_sem.at[0])
        self.settle_ring(self.ag_send, (1, 2))
        for i in SHORT:
            self.reduce_event(i, 2, 2)
            self.reduce_event(i, 1, 0)
        for i in LONG:
            self.reduce_event(i, 2, 4)
            self.reduce_event(i, 1, 0)
        for i in SHORT + LONG:
            self.reduce_event(i, 1, 1)
        for i in SHORT:
            self.reduce_event(i, 1, 2)
        for g in (0, 1):
            self.collect_send(g, "z")
        for i in LONG:
            self.reduce_event(i, 1, 2)
        for g in (0, 1):
            self.collect_send(g, "y")
        self.settle_ring(self.rs_send, (2, 1))
        half = self.gwb.at[:, pl.ds(0, self.shard)]
        for e in range(3):
            self.settle(half, self.g_sem.at[e])
        for a in ("z", "y"):
            for g in (0, 1):
                self.collect_wait(g, a)

    def loss_and_grads(self):
        self.wait_weight()
        acc = self.lg
        acc[...] = jnp.zeros_like(acc)

        @pl.loop(0, NB // BLOCKS)
        def _(b):
            js = [b * BLOCKS + e for e in range(BLOCKS)]
            acc[...] += lax.dot_general(
                jnp.concatenate([self.wv[j] for j in js], axis=1),
                jnp.concatenate([self.hidden_block(j) for j in js], axis=1),
                (((1,), (1,)), ((), ())),
                preferred_element_type=F32,
            )

        swap = (acc, self.lg_in, self.lg_sem.at[0], self.lg_sem.at[1], self.dev(core=1 - self.core))
        self.send(*swap)
        target, scale = self.tgt[...].reshape(1, -1), self.lw[...].reshape(1, -1)
        self.remote(*swap).wait_recv()
        logits = acc[...] + self.lg_in[...]
        self.lg_sum[...] = logits
        row = lax.broadcasted_iota(jnp.int32, logits.shape, 0)
        row = row + jnp.where(row < self.shard, self.vocab0, self.vocab0 + 15 * self.shard)
        hit = row == target
        top = jnp.max(logits, axis=0, keepdims=True)
        total = jnp.sum(jnp.exp(logits - top), axis=0, keepdims=True)
        picked = jnp.sum(jnp.where(hit, logits, 0.0), axis=0, keepdims=True)
        top, total, picked = self.stats(1, self.stats(0, (top, total, picked)))
        lse = top + jnp.log(total)
        self.loss[...] = (lse - picked).reshape(2 * NQ * ROWS)
        dl = scale * (jnp.exp(self.lg_sum[...] - lse) - (row == target).astype(F32))
        self.dlt[...] = dl.astype(BF16)
        self.dlr[...] = dl.T.astype(BF16)

        @pl.loop(0, NB, unroll=BLOCKS)
        def _(j):
            y, zl = j // ZL, lax.rem(j, ZL)
            o = jnp.dot(self.dlr[...], self.wv[j], preferred_element_type=F32)
            for i, (order, off, width) in enumerate(STREAMS):
                for zh in range(ZH):
                    for x in range(4):
                        q = (zh * 4 + x) * 2 * ROWS
                        self.part[i][self.at(order, x, y, zh * ZL + zl)] = o[q : q + 2 * ROWS, off : off + width]

    def stats(self, phase, mine):
        buf = (self.st0, self.st1)[phase]
        sem = (self.st0_sem, self.st1_sem)[phase]
        own = self.me["x"] * 4 + self.me["y"] if phase == 0 else self.me["z"]
        n = buf.shape[0]
        buf[own] = jnp.concatenate(mine + (jnp.zeros((5, 256), F32),), axis=0)

        @pl.loop(1, n)
        def _(e):
            dev = self.dev(x=e // 4, y=lax.rem(e, 4)) if phase == 0 else self.dev(z=e)
            self.send(buf.at[own], buf.at[own], sem.at[0], sem.at[1], dev)

        self.settle_all(buf, sem.at[1], n - 1)
        tiles = [buf[e] for e in range(n)]
        top = tiles[0][0:1]
        for t in tiles[1:]:
            top = jnp.maximum(top, t[0:1])
        total = picked = jnp.zeros_like(top)
        for t in tiles:
            total = total + t[1:2] * jnp.exp(t[0:1] - top)
            picked = picked + t[2:3]
        return (top, total, picked)

    def weight_copies(self, j):
        c, other = self.core, 1 - self.core
        rows = pl.ds(pl.multiple_of(c * self.shard, 16), self.shard)
        cols = lambda h: pl.ds(pl.multiple_of(j * FULL + h * HALF, HALF), HALF)
        dst = self.wv.at[j, rows]
        local = pltpu.make_async_copy(self.w.at[:, cols(c)], dst, self.w_sem.at[0])
        out = lambda: self.remote(
            self.w.at[:, cols(other)], dst, self.w_sem.at[1], self.w_sem.at[2], self.dev(core=other)
        )
        return local, out

    def wait_weight(self):
        half = self.wv.at[:, pl.ds(0, self.shard)]
        for e in range(3):
            self.settle(half, self.w_sem.at[e])

    def grad_weight(self, lo, hi):
        c, other = self.core, 1 - self.core

        @pl.loop(lo, hi, unroll=BLOCKS)
        def _(j):
            self.gwb[j] = jnp.dot(self.dlt[...], self.hidden_block(j), preferred_element_type=F32).astype(BF16)
            src = lambda h: self.gwb.at[j, pl.ds(pl.multiple_of(h * self.shard, 16), self.shard)]
            dst = self.gw.at[:, pl.ds(pl.multiple_of(j * FULL + c * HALF, HALF), HALF)]
            pltpu.make_async_copy(src(c), dst, self.g_sem.at[0]).start()
            self.send(src(other), dst, self.g_sem.at[1], self.g_sem.at[2], self.dev(core=other))

    def run(self):
        other = 1 - self.core
        barrier = pltpu.get_barrier_semaphore()
        peers = [dict(x=dx, y=dy) for dx in range(4) for dy in range(4) if dx or dy]
        peers += [dict(z=dz) for dz in range(1, 8)]
        peers += [dict(core=other, z=dz) for dz in range(8)]
        peers += [dict(core=other, y=dy) for dy in range(1, 4)]
        for d in peers:
            pl.semaphore_signal(barrier, inc=1, device_id=self.dev(**d), device_id_type=MESH)
        for a in ("z", "y"):
            self.spread_own(a).start()

        @pl.loop(0, NB)
        def _(j):
            self.weight_copies(j)[0].start()

        pl.semaphore_wait(barrier, len(peers))
        self.spread()
        self.spread_wait()
        self.gather()
        self.loss_and_grads()
        self.reduce()


def scratch(shard):
    dma = pltpu.SemaphoreType.DMA
    rows = 2 * shard
    out = {
        "wv": pltpu.VMEM((NB, rows, HALF), BF16),
        "lg": pltpu.VMEM((rows, 256), F32),
        "lg_in": pltpu.VMEM((rows, 256), F32),
        "lg_sum": pltpu.VMEM((rows, 256), F32),
        "st0": pltpu.VMEM((16, 8, 256), F32),
        "st1": pltpu.VMEM((8, 8, 256), F32),
        "dlt": pltpu.VMEM((rows, 256), BF16),
        "dlr": pltpu.VMEM((256, rows), BF16),
        "gwb": pltpu.VMEM((NB, rows, HALF), BF16),
        "ag_send": dma((NS, 2)),
        "ag_recv": dma((NS, 2, 2, 2, 4)),
        "rs_send": dma((NS, 2)),
        "rs_recv": dma((NS, 2, 2, 2, 4)),
        "lg_sem": dma((2,)),
        "st0_sem": dma((2,)),
        "st1_sem": dma((2,)),
        "w_sem": dma((3,)),
        "g_sem": dma((3,)),
    }
    for a in ("z", "y"):
        n, width = SIZE[a], WIDE[a][1]
        out[f"first{a}"] = pltpu.VMEM((2, n, ROWS, width), BF16)
        out[f"first_sem{a}"] = dma((2,))
        out[f"last_out{a}"] = pltpu.VMEM((2, n, ROWS, width), F32)
        out[f"last_in{a}"] = pltpu.VMEM((2 * n, ROWS, width), F32)
        out[f"last_sem{a}"] = dma((2, 2))
    for i, (order, _, width) in enumerate(STREAMS):
        l, m, f = lead(order)
        out[f"buf{i}"] = pltpu.VMEM((l, m, f, 2 * ROWS, width), BF16)
        out[f"part{i}"] = pltpu.VMEM((l, m, f, 2 * ROWS, width), F32)
        chunk = {2: (m, f, 2 * ROWS, width), 1: (f, 2 * ROWS, width)}
        for p in (1, 2):
            shape = (2, hops(order, p)) + chunk[p]
            out[f"rs_out{i}{p}"] = pltpu.VMEM(shape, BF16)
            out[f"rs_in{i}{p}"] = pltpu.VMEM(shape, BF16)
    return out


def on_device(hidden, head_weight, targets, loss_weight):
    shard, width = head_weight.shape
    spaces = scratch(shard)

    def body(hid, w, tgt, lw, loss, gw, gh, *refs):
        named = dict(zip(spaces, refs))
        args = dict(hid=hid, w=w, tgt=tgt, lw=lw, loss=loss, gw=gw, gh=gh)
        for kind in ("buf", "part"):
            args[kind] = [named.pop(f"{kind}{i}") for i in range(NS)]
        for kind in ("rs_out", "rs_in"):
            args[kind] = [{p: named.pop(f"{kind}{i}{p}") for p in (1, 2)} for i in range(NS)]
        for kind in ("first", "first_sem", "last_out", "last_in", "last_sem"):
            args[kind] = {a: named.pop(f"{kind}{a}") for a in ("z", "y")}
        args.update(named)
        Kernel(shard, args).run()

    vmem, hbm = pl.BlockSpec(memory_space=pltpu.VMEM), pl.BlockSpec(memory_space=pl.ANY)
    loss, gw, gh = pl.pallas_call(
        body,
        out_shape=(
            pltpu.VMEM(loss_weight.shape, F32),
            pltpu.VMEM((shard, width), BF16),
            pltpu.VMEM(hidden.shape, BF16),
        ),
        in_specs=[hbm, hbm, vmem, vmem],
        out_specs=(vmem, vmem, vmem),
        scratch_shapes=list(spaces.values()),
        compiler_params=pltpu.CompilerParams(
            collective_id=0, has_side_effects=True, vmem_limit_bytes=56 * 1024 * 1024
        ),
        cost_estimate=pl.CostEstimate(
            flops=6 * shard * width * 256, bytes_accessed=4 * shard * width, transcendentals=2 * shard * 512
        ),
    )(hidden, head_weight, targets, loss_weight)
    return (loss, gw, gh)


def solution(mesh):
    in_specs = (P("section", "tensor"), P(("section", "tensor"), None), P(), P())
    out_specs = (P(), P(("section", "tensor"), None), P("section", "tensor"))
    return jax.shard_map(
        on_device, mesh=mesh, in_specs=in_specs, out_specs=out_specs, check_vma=False
    )
```
